32 devices in a mesh: groups: 2 (over y), row: 16 (over z, x, core).
Axes of the slice: x: 2, y: 2, z: 4, core: 2. Of those that a mesh axis runs over, the one named last changes fastest.
Arguments:
- aligned_activations: bfloat16 [160, 128, 256], P('groups', 'row'), parts along dimension 0, may hold values from -6 to 6
- standardizer_scale: float32 [256], replicated, may hold values from 0.5 to 1.5
- standardizer_shift: float32 [256], replicated, may hold values from -3 to 3
- factor_matrices: bfloat16 [256, 64], replicated, may hold values from -0.375 to 0.375
- factor_shift: float32 [64], replicated, may hold values from -3 to 3
- final_matrix: bfloat16 [1024, 128], replicated, may hold values from -0.1875 to 0.1875
- final_shift: float32 [128], replicated, may hold values from -3 to 3
- interaction_adjoint: bfloat16 [256, 128, 128], P(('groups', 'row')), parts along dimension 0, may hold values from -6 to 6
- polymer_lengths: int32 [24], P('groups'), parts along dimension 0, may hold values from 1 to 32, 128 in all
- lone_homolog_numbers: int32 [24], P('groups'), parts along dimension 0, may hold values from 1 to 8, 48 in all
Outputs:
- pair_delta: bfloat16 [256, 128, 128], P(('groups', 'row')), parts along dimension 0
- alignment_gradient: bfloat16 [160, 128, 256], P('groups', 'row'), parts along dimension 0
- output_weight_gradient: float32 [2048, 128], P('groups'), parts along dimension 0
- factor_matrices_adjoint: float32 [512, 64], P('groups'), parts along dimension 0
The draws below stay inside these ranges and needn't reach their ends.
There are 2 independent parts, one for each index of `groups`. The reference program is written for one: setup_inputs(seed, part) draws one part's arguments, and reference() takes and returns one part's arrays. A program takes and returns all parts, laid end to end along the dimension named above; an argument that names none is the same for every part. Nothing has to cross between parts.
Inputs may be any that keep to these rules, and one draw needn't show every extreme that they name: `polymer_lengths`: each chain has at least one residue; the chains' lengths sum to 128; the longest has exactly 32. `lone_homolog_numbers`: each chain has at least one unpaired row; the counts sum to 48; the largest is exactly 8.
All inputs are finite; a program needn't handle non-finite values.
Results may differ from the reference program's by a relative error of at most 0.0069.
Values may be sent and summed in bfloat16 or wider, within the bound.
No kernel may reach another device: no remote copies, remote signals or barrier semaphores. Data moves between devices by JAX's collectives and lax.ppermute only.
A program may use at most 192 MiB of HBM per device.

```python
import math
import jax
import jax.numpy as jnp
import numpy as np
from jax import lax

FEATURE_DEPTH = 256
FACTOR_RANK = 32
Z = 128
P_SIZE = 32
U = 48
CHAINS = 12
ALIGNED_DEPTH = 80
SITE_NUMBER = 128


def levels(stream_key, dims, pieces, low, high):
    loudness = 1.0
    for dim, shards_of in pieces:
        heights = jax.random.uniform(jax.random.fold_in(jax.random.fold_in(stream_key, 6), dim), (shards_of,), jnp.float32, low / len(pieces), high / len(pieces))
        loudness = loudness * jnp.repeat(jnp.exp(heights), dims[dim] // shards_of).reshape((-1,) + (1,) * (len(dims) - 1 - dim))
    return loudness


def profile(count, total, reach, lean):
    loads = [(1 << 20) // math.isqrt(rank ** lean) + 1 for rank in range(2, count + 1)]
    spare, given = total - reach - (count - 1), [1] * (count - 1)
    while spare > 0:
        free = [i for i in range(count - 1) if given[i] < reach]
        pool, remaining = sum([loads[i] for i in free]), spare
        for i in free:
            addition = min(reach - given[i], max(1, remaining * loads[i] // pool), spare)
            given[i] = given[i] + addition
            spare = spare - addition
    return np.array([reach] + given)


def ragged_sizes(rng, number_of, total, most, skew):
    if number_of == 2:
        one = jax.random.randint(rng, (), max(1, total - most), min(most, total - 1) + 1)
        return jnp.stack([one, total - one])
    lengths = jnp.asarray(profile(number_of, total, most, skew), jnp.int32)
    twos = (number_of - 1) // 2
    giver, receiver = lengths[1:1 + 2 * twos:2], lengths[2:2 + 2 * twos:2]
    margin = jnp.minimum(giver - 1, most - receiver)
    shifted = jax.random.randint(jax.random.fold_in(rng, 1), (twos,), 0, 1 << 20) % (margin + 1)
    lengths = lengths.at[1:1 + 2 * twos:2].set(giver - shifted).at[2:2 + 2 * twos:2].set(receiver + shifted)
    return lengths[jax.random.permutation(jax.random.fold_in(rng, 2), number_of)]


def noise(rng, extent, scale, reach, split=(), held_as=jnp.bfloat16):
    level = levels(rng, extent, split, -0.22, 0.18) if split else 1.0
    entries = jax.random.normal(rng, extent, jnp.float32) * scale * level
    return jnp.minimum(jnp.maximum(entries, -reach), reach).astype(held_as)


def setup_inputs(seed: int = 0, part: int = 0) -> dict:
    seeds = jax.random.split(jax.random.key(seed), 11)
    part_keys = jax.random.split(jax.random.fold_in(seeds[10], part), 11)
    return {
        "aligned_activations": noise(part_keys[0], (ALIGNED_DEPTH, SITE_NUMBER, FEATURE_DEPTH), 1.0, 6.0, ((1, 16),)),
        "standardizer_scale": jnp.clip(1.0 + 0.1 * jax.random.normal(seeds[1], (FEATURE_DEPTH,), jnp.float32), 0.5, 1.5),
        "standardizer_shift": noise(seeds[2], (FEATURE_DEPTH,), 0.5, 3.0, (), jnp.float32),
        "factor_matrices": noise(seeds[3], (FEATURE_DEPTH, 2 * FACTOR_RANK), FEATURE_DEPTH ** -0.5, 0.375),
        "factor_shift": noise(seeds[4], (2 * FACTOR_RANK,), 0.5, 3.0, (), jnp.float32),
        "final_matrix": noise(seeds[5], (FACTOR_RANK * FACTOR_RANK, Z), (FACTOR_RANK * FACTOR_RANK) ** -0.5, 0.1875),
        "final_shift": noise(seeds[6], (Z,), 0.5, 3.0, (), jnp.float32),
        "interaction_adjoint": noise(part_keys[7], (SITE_NUMBER, SITE_NUMBER, Z), 1.0, 6.0, ((0, 16),)),
        "polymer_lengths": ragged_sizes(part_keys[8], CHAINS, SITE_NUMBER, SITE_NUMBER // 4, 2).astype(jnp.int32),
        "lone_homolog_numbers": ragged_sizes(part_keys[9], CHAINS, U, U // 6, 2).astype(jnp.int32),
    }


def chain_tables(polymer_lengths, lone_homolog_numbers, residue_ids, unpaired_ids):
    bounds = jnp.cumsum(polymer_lengths, dtype=jnp.int32)
    res_chain = lax.optimization_barrier(jnp.sum((residue_ids[:, None] >= bounds[None, :]).astype(jnp.int32), axis=1, dtype=jnp.int32))
    row_bounds = jnp.cumsum(lone_homolog_numbers, dtype=jnp.int32)
    row_chain = lax.optimization_barrier(jnp.sum((unpaired_ids[:, None] >= row_bounds[None, :]).astype(jnp.int32), axis=1, dtype=jnp.int32))
    return (res_chain, row_chain)

def build_mask(res_chain, row_chain):
    paired = jnp.ones((P_SIZE, res_chain.shape[0]), jnp.float32)
    blocked = (row_chain[:, None] == res_chain[None, :]).astype(jnp.float32)
    return jnp.concatenate([paired, blocked], axis=0)

def unpaired_of(res_chain, lone_homolog_numbers):
    chain_ids = jnp.arange(CHAINS, dtype=jnp.int32)
    picked = jnp.where(res_chain[:, None] == chain_ids[None, :], lone_homolog_numbers[None, :], 0)
    return lax.optimization_barrier(jnp.sum(picked, axis=1)).astype(jnp.float32)

def pair_count(chain_rows, unpaired_rows, chain_cols):
    same_chain = chain_rows[:, None] == chain_cols[None, :]
    return jnp.float32(P_SIZE) + jnp.where(same_chain, unpaired_rows[:, None], jnp.float32(0.0)) + jnp.float32(0.001)

def standardize_features(entry_tensor, standardizer_scale, standardizer_shift):
    average = lax.optimization_barrier(jnp.mean(entry_tensor, axis=-1, keepdims=True))
    centred = entry_tensor - average
    spread = lax.optimization_barrier(jnp.mean(centred * centred, axis=-1, keepdims=True))
    return centred * lax.rsqrt(spread + 1e-05) * standardizer_scale + standardizer_shift

def reference(aligned_activations, standardizer_scale, standardizer_shift, factor_matrices, factor_shift, final_matrix, final_shift, interaction_adjoint, polymer_lengths, lone_homolog_numbers):
    res_chain, row_chain = chain_tables(polymer_lengths, lone_homolog_numbers, jnp.arange(SITE_NUMBER, dtype=jnp.int32), jnp.arange(U, dtype=jnp.int32))
    row_mask = build_mask(res_chain, row_chain)
    unpaired_res = unpaired_of(res_chain, lone_homolog_numbers)
    standardized_entry, standardize_reverse = jax.vjp(lambda entry_tensor: standardize_features(entry_tensor, standardizer_scale, standardizer_shift), aligned_activations.astype(jnp.float32))
    standardized_matrix = standardized_entry.astype(jnp.bfloat16)
    factor_vectors = jnp.dot(standardized_matrix.reshape(ALIGNED_DEPTH * SITE_NUMBER, FEATURE_DEPTH), factor_matrices, preferred_element_type=jnp.float32) + factor_shift
    factor_vectors = (factor_vectors.reshape(ALIGNED_DEPTH, SITE_NUMBER, 2 * FACTOR_RANK) * row_mask[:, :, None]).astype(jnp.bfloat16)
    left_float = factor_vectors[:, :, :FACTOR_RANK].astype(jnp.float32)
    right_float = factor_vectors[:, :, FACTOR_RANK:].astype(jnp.float32)
    block_rows = 32

    def row_block(carried, block_index):
        out_acc, right_acc = carried
        block_start = (block_index * block_rows).astype(jnp.int32)
        left_block = lax.dynamic_slice_in_dim(left_float, block_start, block_rows, 1)
        chain_rows = lax.dynamic_slice_in_dim(res_chain, block_start, block_rows, 0)
        unpaired_rows = lax.dynamic_slice_in_dim(unpaired_res, block_start, block_rows, 0)
        counts = pair_count(chain_rows, unpaired_rows, res_chain)
        outer_block = jnp.einsum('sic,sjd->ijcd', left_block, right_float).astype(jnp.bfloat16).reshape(block_rows * SITE_NUMBER, FACTOR_RANK * FACTOR_RANK)
        pair_block = jnp.dot(outer_block, final_matrix, preferred_element_type=jnp.float32).reshape(block_rows, SITE_NUMBER, Z) + final_shift
        pair_block = (pair_block / counts[:, :, None]).astype(jnp.bfloat16)
        cot_block = lax.dynamic_slice_in_dim(interaction_adjoint, block_start, block_rows, 0)
        scaled = (cot_block.astype(jnp.float32) / counts[:, :, None]).astype(jnp.bfloat16)
        scaled_flat = scaled.reshape(block_rows * SITE_NUMBER, Z)
        out_acc = out_acc + jnp.dot(outer_block.T, scaled_flat, preferred_element_type=jnp.float32)
        outer_grad = jnp.dot(scaled_flat, final_matrix.T, preferred_element_type=jnp.float32).astype(jnp.bfloat16)
        outer_grad = outer_grad.reshape(block_rows, SITE_NUMBER, FACTOR_RANK, FACTOR_RANK).astype(jnp.float32)
        left_grad_block = jnp.einsum('ijcd,sjd->sic', outer_grad, right_float)
        right_acc = right_acc + jnp.einsum('ijcd,sic->sjd', outer_grad, left_block)
        return ((out_acc, right_acc), (pair_block, left_grad_block))
    start_carry = (jnp.zeros((FACTOR_RANK * FACTOR_RANK, Z), jnp.float32), jnp.zeros((ALIGNED_DEPTH, SITE_NUMBER, FACTOR_RANK), jnp.float32))
    (output_weight_gradient, right_grad), (pair_blocks, left_blocks) = lax.scan(row_block, start_carry, jnp.arange(SITE_NUMBER // block_rows, dtype=jnp.int32))
    pair_delta = pair_blocks.reshape(SITE_NUMBER, SITE_NUMBER, Z)
    left_grad = jnp.transpose(left_blocks, (1, 0, 2, 3)).reshape(ALIGNED_DEPTH, SITE_NUMBER, FACTOR_RANK)
    factor_sensitivity = (jnp.concatenate([left_grad, right_grad], axis=2) * row_mask[:, :, None]).astype(jnp.bfloat16)
    factor_matrices_adjoint = jnp.dot(standardized_matrix.reshape(ALIGNED_DEPTH * SITE_NUMBER, FEATURE_DEPTH).T, factor_sensitivity.reshape(ALIGNED_DEPTH * SITE_NUMBER, 2 * FACTOR_RANK), preferred_element_type=jnp.float32)
    standardized_sensitivity = jnp.dot(factor_sensitivity.reshape(ALIGNED_DEPTH * SITE_NUMBER, 2 * FACTOR_RANK), factor_matrices.T, preferred_element_type=jnp.float32).reshape(ALIGNED_DEPTH, SITE_NUMBER, FEATURE_DEPTH)
    alignment_gradient = standardize_reverse(standardized_sensitivity)[0].astype(jnp.bfloat16)
    return (pair_delta, alignment_gradient, output_weight_gradient, factor_matrices_adjoint)
```

```python
import jax
import jax.numpy as jnp
from jax import lax
from jax.experimental import pallas as pl
from jax.experimental.pallas import tpu as pltpu
from jax.sharding import PartitionSpec as P

PAIRED = 32
EXTRA = 8
QUAD = 4
BLOCK = 8
RANK = 32
PACKED = 80
F32 = jnp.float32
BF16 = jnp.bfloat16
SMEM = pl.BlockSpec(memory_space=pltpu.SMEM)


def vmem():
    return pl.BlockSpec(memory_space=pltpu.VMEM)


def params(mib=48):
    return pltpu.CompilerParams(vmem_limit_bytes=mib * 1024 * 1024)


def sds(shape, dtype):
    return jax.ShapeDtypeStruct(shape, dtype)


def place():
    k = lax.axis_index("row")
    return k >> 2, k & 3


def bounds_of(ref):
    ends, total = [], jnp.int32(0)
    for c in range(ref.shape[0]):
        total = total + ref[c]
        ends.append(total)
    return ends


def chain_of(residue, ends):
    chain = jnp.zeros(residue.shape, jnp.int32)
    for end in ends:
        chain = chain + jnp.where(residue >= end, 1, 0)
    return chain


def count_of(chain, hom_ref):
    picked = jnp.zeros(chain.shape, F32)
    for c in range(hom_ref.shape[0]):
        picked = jnp.where(chain == c, hom_ref[c].astype(F32), picked)
    return picked


def swap4(xs, low):
    lane = lax.broadcasted_iota(jnp.int32, xs[0].shape, 1)
    for bit, step in ((2, 2 * low), (1, low)):
        keep = (lane & step) == 0
        ys = list(xs)
        for q in range(4):
            if q & bit == 0:
                lo, hi = xs[q], xs[q | bit]
                ys[q] = jnp.where(keep, lo, pltpu.roll(hi, step, 1))
                ys[q | bit] = jnp.where(keep, pltpu.roll(lo, 128 - step, 1), hi)
        xs = ys
    return xs


def unpack(message):
    m = message.astype(F32)
    return [
        jnp.concatenate([m[0:32], m[64:72]], axis=0),
        jnp.concatenate([m[32:64], m[72:80]], axis=0),
    ]


def pack(lo, hi):
    return jnp.concatenate([lo[0:32], hi[0:32], lo[32:40], hi[32:40]], axis=0).astype(BF16)


def spread_rows(compact, chain, chains):
    rows = [compact[0:PAIRED]]
    extra = compact[PAIRED:]
    for c in range(chains):
        rows.append(jnp.where(chain == c, extra, 0.0))
    return jnp.concatenate(rows, axis=0)


def gather_rows(full, chain, chains):
    extra = jnp.zeros((EXTRA, full.shape[1]), F32)
    for c in range(chains):
        top = PAIRED + EXTRA * c
        extra = jnp.where(chain == c, full[top : top + EXTRA], extra)
    return jnp.concatenate([full[0:PAIRED], extra], axis=0)


def left_chain(a, b, ends):
    lane = lax.broadcasted_iota(jnp.int32, (EXTRA, 128), 1)
    residue = 32 * a + 8 * (b ^ (lane >> 5)) + (lane & 7)
    return jnp.concatenate([chain_of(residue, ends)] * 8, axis=1)


def right_chain(a, b, chunk, ends):
    lane = lax.broadcasted_iota(jnp.int32, (EXTRA, 256), 1)
    parts = []
    for tt in range(4):
        residue = 32 * (a ^ (4 * chunk + tt)) + 8 * b + (lane >> 5)
        parts.append(chain_of(residue, ends))
    return jnp.concatenate(parts, axis=1)


def spread_matrix():
    row = lax.broadcasted_iota(jnp.int32, (512, 512), 0)
    o = lax.broadcasted_iota(jnp.int32, (512, 512), 1)
    r, k = row >> 6, row & 63
    target = jnp.where(k < RANK, k * 8 + r, 256 + r * 32 + (k - RANK))
    return jnp.where(o == target, 1.0, 0.0).astype(BF16)


def cut_kernel(adj_ref, *refs):
    outs, work = refs[:QUAD], refs[QUAD]
    residues = adj_ref.shape[1]
    groups = residues // 32
    a, b = place()
    work[...] = adj_ref[...].astype(F32).reshape(BLOCK * residues, 128)
    for t in range(QUAD):

        def step(u, _, t=t):
            tiles = []
            for jj in range(BLOCK):
                j = 32 * (a ^ u) + 8 * (b ^ t) + jj
                tiles.append(work[pl.ds(j, BLOCK, stride=residues), :])
            rows = pl.ds(pl.multiple_of(u * 64, 64), 64)
            outs[t][rows, :] = jnp.concatenate(tiles, axis=0).astype(BF16)
            return 0

        lax.fori_loop(0, groups, step, 0, unroll=groups <= 4)


def project_kernel(
    x_ref, scale_ref, shift_ref, mat_ref, off_ref, len_ref, hom_ref,
    left_ref, right_ref, norm_ref, hat_ref, rstd_ref, spread_ref, full, comp,
):
    depth = x_ref.shape[0]
    chains = len_ref.shape[0]
    a, b = place()
    x = x_ref[...].astype(F32)
    centred = x - jnp.mean(x, axis=-1, keepdims=True)
    rstd = lax.rsqrt(jnp.mean(centred * centred, axis=-1, keepdims=True) + 1e-05)
    hat = (centred * rstd).reshape(depth * BLOCK, 256)
    normed = (hat * scale_ref[...] + shift_ref[...]).astype(BF16)
    hat_ref[...] = hat
    norm_ref[...] = normed
    rstd_ref[...] = jnp.broadcast_to(rstd, (depth, BLOCK, 128)).reshape(depth * BLOCK, 128)
    proj = jnp.dot(normed, mat_ref[...], preferred_element_type=F32) + off_ref[...]
    full[0 : depth * BLOCK, :] = proj
    full[depth * BLOCK :, :] = jnp.zeros((EXTRA * BLOCK, 64), F32)
    comp[0 : PAIRED * BLOCK, :] = proj[0 : PAIRED * BLOCK]
    residue = lax.broadcasted_iota(jnp.int32, (EXTRA * BLOCK, 64), 0)
    entry = residue >> 3
    chain = chain_of(32 * a + 8 * b + (residue & 7), bounds_of(len_ref))
    extra = jnp.zeros((EXTRA * BLOCK, 64), F32)
    start = jnp.int32(PAIRED)
    for c in range(chains):
        rows = full[pl.ds(pl.multiple_of(start * BLOCK, BLOCK), EXTRA * BLOCK), :]
        extra = jnp.where((chain == c) & (entry < hom_ref[c]), rows, extra)
        start = start + hom_ref[c]
    comp[PAIRED * BLOCK :, :] = extra
    rows = PAIRED + EXTRA
    wide = jnp.concatenate([comp[pl.ds(r, rows, stride=BLOCK), :] for r in range(BLOCK)], axis=1)
    spread = spread_matrix()
    spread_ref[...] = spread
    out = jnp.dot(wide.astype(BF16), spread, preferred_element_type=F32)
    left_ref[...] = pack(out[:, 0:128], out[:, 128:256])
    right_ref[...] = pack(out[:, 256:384], out[:, 384:512])


def adjoint_kernel(len_ref, hom_ref, final_ref, *refs):
    pieces, (s_ref, og_ref, ft_ref) = refs[:QUAD], refs[QUAD:]
    chunk = pl.program_id(0)
    a, b = place()
    ends = bounds_of(len_ref)
    low = lax.broadcasted_iota(jnp.int32, (32, 128), 0)
    chain_i, inv_same = [], []
    for t in range(QUAD):
        chain = chain_of(32 * a + 8 * (b ^ t) + (low & 7), ends)
        chain_i.append(chain)
        inv_same.append(1.0 / (float(PAIRED) + count_of(chain, hom_ref) + 0.001))
    inv_other = 1.0 / jnp.full((32, 128), PAIRED + 0.001, F32)
    blocks = []
    for tt in range(4):
        for half in range(2):
            chain_j = chain_of(32 * (a ^ (4 * chunk + tt)) + 8 * b + 4 * half + (low >> 3), ends)
            top = tt * 64 + half * 32
            for t in range(QUAD):
                inv = jnp.where(chain_i[t] == chain_j, inv_same[t], inv_other)
                blocks.append(pieces[t][top : top + 32, :].astype(F32) * inv)
    s = jnp.concatenate(blocks, axis=0).astype(BF16)
    s_ref[...] = s
    ft_ref[...] = final_ref[...].astype(F32).T.astype(BF16)
    for cb in range(8):
        og = lax.dot_general(
            final_ref[cb * 128 : cb * 128 + 128, :], s, (((1,), (1,)), ((), ())),
            preferred_element_type=F32,
        ).astype(BF16)
        for jg in range(8):
            xs = [og[cl * 32 : cl * 32 + 32, jg * 128 : jg * 128 + 128] for cl in range(4)]
            ys = swap4(xs, 8)
            for jl in range(4):
                top = (jg * 4 + jl) * 32
                og_ref[top : top + 32, cb * 128 : cb * 128 + 128] = ys[jl]


def left_lanes(lefts):
    parts = [unpack(m[...]) for m in lefts]
    lanes = []
    for h in range(2):
        lanes += swap4([parts[t][h] for t in range(QUAD)], 32)
    return jnp.concatenate(lanes, axis=1)


def right_lanes(rights):
    return jnp.concatenate([blk for m in rights for blk in unpack(m[...])], axis=1)


def grad_kernel(len_ref, og_ref, *refs):
    lefts, rights = refs[0:4], refs[4:8]
    lg_refs, rg_refs = refs[8:12], refs[12:16]
    lx_ref, rt_ref, acc = refs[16:19]
    chains = len_ref.shape[0]
    chunk, chunks = pl.program_id(0), pl.num_programs(0)
    a, b = place()
    ends = bounds_of(len_ref)
    chain_l = left_chain(a, b, ends)
    chain_r = right_chain(a, b, chunk, ends)
    lx = spread_rows(left_lanes(lefts), chain_l, chains).astype(BF16)
    rx = spread_rows(right_lanes(rights), chain_r, chains)
    lx_ref[...] = lx
    rt_ref[...] = rx.T.astype(BF16)
    og = og_ref[...]
    lg = jnp.dot(rx.astype(BF16), og, preferred_element_type=F32)
    rg = lax.dot_general(lx, og, (((1,), (1,)), ((), ())), preferred_element_type=F32)
    rg = gather_rows(rg, chain_r, chains)
    for tt in range(4):
        rg_refs[tt][...] = pack(rg[:, tt * 256 : tt * 256 + 128], rg[:, tt * 256 + 128 : tt * 256 + 256])

    @pl.when(chunk == 0)
    def _():
        acc[...] = lg

    @pl.when(chunk > 0)
    def _():
        acc[...] += lg

    @pl.when(chunk == chunks - 1)
    def _():
        lgc = gather_rows(acc[...], chain_l, chains)
        halves = []
        for h in range(2):
            xs = [lgc[:, (4 * h + q) * 128 : (4 * h + q + 1) * 128] for q in range(4)]
            halves.append(swap4(xs, 32))
        for t in range(QUAD):
            lg_refs[t][...] = pack(halves[0][t], halves[1][t])


def outer_kernel(len_ref, hom_ref, lx_ref, rt_ref, s_ref, ft_ref, bias_ref, *refs):
    pair_refs, w_refs = refs[0:4], refs[4:8]
    n_buf, acc = refs[8:10]
    chunk, chunks = pl.program_id(0), pl.num_programs(0)
    a, b = place()
    ends = bounds_of(len_ref)
    lx = lx_ref[...]
    for jg in range(8):
        o = jnp.dot(rt_ref[jg * 128 : jg * 128 + 128, :], lx, preferred_element_type=F32).astype(BF16)
        for cb in range(8):
            xs = [o[jl * 32 : jl * 32 + 32, cb * 128 : cb * 128 + 128] for jl in range(4)]
            ys = swap4(xs, 8)
            for cl in range(4):
                top = (cb * 4 + cl) * 32
                n_buf[top : top + 32, jg * 128 : jg * 128 + 128] = ys[cl]
    n = n_buf[...]
    w = jnp.dot(n, s_ref[...], preferred_element_type=F32)

    @pl.when(chunk == 0)
    def _():
        acc[...] = w

    @pl.when(chunk > 0)
    def _():
        acc[...] += w

    @pl.when(chunk == chunks - 1)
    def _():
        for t in range(QUAD):
            rows = pl.ds(pl.multiple_of((b ^ t) * 256, 256), 256)
            w_refs[t][...] = acc[rows, :].astype(BF16)

    pt = jnp.dot(ft_ref[...], n, preferred_element_type=F32)
    lane = lax.broadcasted_iota(jnp.int32, (8, 128), 1)
    res_i = 32 * a + 8 * (b ^ (lane >> 5)) + (lane & 7)
    chain_i = chain_of(res_i, ends)
    same_inv = 1.0 / (float(PAIRED) + count_of(chain_i, hom_ref) + 0.001)
    other_inv = 1.0 / jnp.full((8, 128), PAIRED + 0.001, F32)
    bias = bias_ref[...]
    tiles = []
    for tt in range(4):
        for half in range(2):
            res_j = 32 * (a ^ (4 * chunk + tt)) + 8 * b + 4 * half + ((lane >> 3) & 3)
            inv = jnp.where(chain_i == chain_of(res_j, ends), same_inv, other_inv)
            inv_col = jnp.broadcast_to(inv[0:1], (128, 128)).T
            blk = tt * 2 + half
            tiles.append((pt[:, blk * 128 : blk * 128 + 128].T + bias) * inv_col)
    for t in range(QUAD):
        pair_refs[t][...] = jnp.concatenate([x[t * 32 : t * 32 + 32] for x in tiles], axis=0).astype(BF16)


def total(refs):
    out = refs[0][...].astype(F32)
    for ref in refs[1:]:
        out = out + ref[...].astype(F32)
    return out


def sum_kernel(*refs):
    refs[-1][...] = total(refs[:-1]).astype(BF16)


def back_kernel(quad, groups, len_ref, hom_ref, spread_ref, norm_ref, *refs):
    lgs, rgs = refs[:quad], refs[quad : quad + groups]
    pg_ref, fm_ref, comp, full = refs[quad + groups :]
    chains = len_ref.shape[0]
    depth8 = pg_ref.shape[0]
    a, b = place()
    lg, rg = total(lgs), total(rgs)
    wide = jnp.concatenate(
        [blk for g in (lg, rg) for blk in unpack(g)], axis=1
    ).astype(BF16)
    rows = PAIRED + EXTRA
    per = lax.dot_general(
        wide, spread_ref[...], (((1,), (1,)), ((), ())), preferred_element_type=F32
    )
    for r in range(BLOCK):
        comp[pl.ds(r, rows, stride=BLOCK), :] = per[:, r * 64 : r * 64 + 64]
    full[0 : PAIRED * BLOCK, :] = comp[0 : PAIRED * BLOCK, :]
    full[PAIRED * BLOCK :, :] = jnp.zeros((full.shape[0] - PAIRED * BLOCK, 64), F32)
    extra = comp[PAIRED * BLOCK :, :]
    residue = lax.broadcasted_iota(jnp.int32, (EXTRA * BLOCK, 64), 0)
    entry = residue >> 3
    chain = chain_of(32 * a + 8 * b + (residue & 7), bounds_of(len_ref))
    start = jnp.int32(PAIRED)
    for c in range(chains):
        at = pl.ds(pl.multiple_of(start * BLOCK, BLOCK), EXTRA * BLOCK)
        full[at, :] += jnp.where((chain == c) & (entry < hom_ref[c]), extra, 0.0)
        start = start + hom_ref[c]
    pg = full[0:depth8, :]
    pg_ref[...] = pg.astype(BF16)
    fm = jnp.dot(pg.T.astype(BF16), norm_ref[...], preferred_element_type=F32)
    fm_ref[...] = jnp.concatenate([fm[:, 0:128], fm[:, 128:256]], axis=0).astype(BF16)


def align_kernel(pg_ref, mat_ref, scale_ref, hat_ref, rstd_ref, out_ref):
    g = lax.dot_general(
        pg_ref[...], mat_ref[...], (((1,), (1,)), ((), ())), preferred_element_type=F32
    )
    g = g * scale_ref[...]
    hat = hat_ref[...]
    m1 = jnp.mean(g, axis=-1, keepdims=True)
    m2 = jnp.mean(g * hat, axis=-1, keepdims=True)
    rstd = rstd_ref[...]
    dx = (g - m1 - hat * m2) * jnp.concatenate([rstd, rstd], axis=1)
    out_ref[...] = dx.reshape(out_ref.shape).astype(BF16)


def pair_kernel(*refs):
    pieces, out_ref, work = refs[:QUAD], refs[QUAD], refs[QUAD + 1]
    residues = out_ref.shape[1]
    groups = residues // 32
    a, b = place()
    for t in range(QUAD):

        def step(u, _, t=t):
            tile = pieces[t][pl.ds(pl.multiple_of(u * 64, 64), 64), :].astype(F32)
            for jj in range(BLOCK):
                j = 32 * (a ^ u) + 8 * (b ^ t) + jj
                work[pl.ds(j, BLOCK, stride=residues), :] = tile[jj * 8 : jj * 8 + 8]
            return 0

        lax.fori_loop(0, groups, step, 0, unroll=groups <= 4)
    out_ref[...] = work[...].reshape(out_ref.shape).astype(BF16)


def merge_kernel(groups, *refs):
    out_ref = refs[-1]
    out_ref[0:256, :] = total(refs[:groups]).astype(BF16)
    out_ref[256:384, :] = total(refs[groups : 2 * groups]).astype(BF16)


def final_kernel(m0, m1, m2, m3, w_ref, fm_ref):
    _, b = place()
    fm = jnp.zeros((128, 128), F32)
    for t, m in enumerate((m0, m1, m2, m3)):
        rows = pl.ds(pl.multiple_of((b ^ t) * 256, 256), 256)
        w_ref[rows, :] = m[0:256, :].astype(F32)
        fm = fm + m[256:384, :].astype(F32)
    fm_ref[0:128, :] = fm[0:64].T
    fm_ref[128:256, :] = fm[64:128].T


def call(kernel, outs, ins, in_specs=None, scratch=(), **kw):
    many = isinstance(outs, (list, tuple))
    return pl.pallas_call(
        kernel,
        out_shape=outs,
        in_specs=in_specs if in_specs is not None else [vmem()] * len(ins),
        out_specs=[vmem()] * len(outs) if many else vmem(),
        scratch_shapes=list(scratch),
        compiler_params=params(),
        **kw,
    )(*ins)


def on_device(
    devices, x, scale, shift, mat, off, final, bias, adjoint, lengths, homologs
):
    groups = devices // QUAD
    chunks = groups // 4
    residues = adjoint.shape[1]
    depth = x.shape[0]
    scale, shift, off, bias = scale[None], shift[None], off[None], bias[None]

    def near(value, t):
        return lax.ppermute(value, "row", [(k, k ^ t) for k in range(devices)])

    def far(value, u):
        return lax.ppermute(value, "row", [(k, k ^ (4 * u)) for k in range(devices)])

    pieces = call(
        cut_kernel,
        [sds((groups * 64, 128), BF16)] * QUAD,
        [adjoint],
        scratch=[pltpu.VMEM((BLOCK * residues, 128), F32)],
    )
    pieces = [pieces[0]] + [near(pieces[t], t) for t in range(1, QUAD)]

    left, right, normed, hat, rstd, spread = call(
        project_kernel,
        [
            sds((PACKED, 128), BF16),
            sds((PACKED, 128), BF16),
            sds((depth * BLOCK, 256), BF16),
            sds((depth * BLOCK, 256), F32),
            sds((depth * BLOCK, 128), F32),
            sds((512, 512), BF16),
        ],
        [x, scale, shift, mat, off, lengths, homologs],
        in_specs=[vmem()] * 5 + [SMEM] * 2,
        scratch=[
            pltpu.VMEM(((depth + EXTRA) * BLOCK, 64), F32),
            pltpu.VMEM(((PAIRED + EXTRA) * BLOCK, 64), F32),
        ],
    )
    lefts = [left] + [near(left, t) for t in range(1, QUAD)]
    rights = [right] + [far(right, u) for u in range(1, groups)]

    def by_slot(parts):
        if chunks == 1:
            return parts
        return [jnp.concatenate(parts[s::4], axis=0) for s in range(4)]

    def from_slot(parts, rows):
        return [parts[u % 4][(u // 4) * rows : (u // 4 + 1) * rows] for u in range(groups)]

    rights = by_slot(rights)

    def rows_of(rows, lanes):
        return pl.BlockSpec((rows, lanes), lambda g: (g, 0))

    def whole(rows, lanes):
        return pl.BlockSpec((rows, lanes), lambda g: (0, 0))

    s, og, final_t = pl.pallas_call(
        adjoint_kernel,
        grid=(chunks,),
        out_shape=[
            sds((chunks * 1024, 128), BF16),
            sds((chunks * 1024, 1024), BF16),
            sds((128, 1024), BF16),
        ],
        in_specs=[SMEM, SMEM, whole(1024, 128)] + [rows_of(256, 128)] * QUAD,
        out_specs=[rows_of(1024, 128), rows_of(1024, 1024), whole(128, 1024)],
        compiler_params=params(),
    )(lengths, homologs, final, *pieces)

    grads = pl.pallas_call(
        grad_kernel,
        grid=(chunks,),
        out_shape=[sds((PACKED, 128), BF16)] * QUAD
        + [sds((chunks * PACKED, 128), BF16)] * 4
        + [sds((128, 1024), BF16), sds((chunks * 1024, 128), BF16)],
        in_specs=[SMEM, rows_of(1024, 1024)]
        + [whole(PACKED, 128)] * QUAD
        + [rows_of(PACKED, 128)] * 4,
        out_specs=[whole(PACKED, 128)] * QUAD
        + [rows_of(PACKED, 128)] * 4
        + [whole(128, 1024), rows_of(1024, 128)],
        scratch_shapes=[pltpu.VMEM((128, 1024), F32)],
        compiler_params=params(),
    )(lengths, og, *lefts, *rights)
    lgs, rgs, (lx, rt) = grads[0:4], grads[4:8], grads[8:10]
    rgs = list(rgs) if chunks == 1 else from_slot(rgs, PACKED)
    lgs = [lgs[0]] + [near(lgs[t], t) for t in range(1, QUAD)]
    rgs = [rgs[0]] + [far(rgs[u], u) for u in range(1, groups)]

    outs = pl.pallas_call(
        outer_kernel,
        grid=(chunks,),
        out_shape=[sds((groups * 64, 128), BF16)] * QUAD + [sds((256, 128), BF16)] * QUAD,
        in_specs=[SMEM, SMEM, whole(128, 1024), rows_of(1024, 128), rows_of(1024, 128)]
        + [whole(128, 1024), whole(1, 128)],
        out_specs=[rows_of(256, 128)] * QUAD + [whole(256, 128)] * QUAD,
        scratch_shapes=[pltpu.VMEM((1024, 1024), BF16), pltpu.VMEM((1024, 128), F32)],
        compiler_params=params(),
    )(lengths, homologs, lx, rt, s, final_t, bias)
    pairs, ws = outs[0:4], outs[4:8]
    ws = [ws[0]] + [near(ws[t], t) for t in range(1, QUAD)]
    pairs = [pairs[0]] + [near(pairs[t], t) for t in range(1, QUAD)]
    w_quad = call(sum_kernel, sds((256, 128), BF16), ws)
    w_quads = [w_quad] + [far(w_quad, u) for u in range(1, groups)]

    pg, fm = call(
        lambda *refs: back_kernel(QUAD, groups, *refs),
        [sds((depth * BLOCK, 64), BF16), sds((128, 128), BF16)],
        [lengths, homologs, spread, normed, *lgs, *rgs],
        in_specs=[SMEM] * 2 + [vmem()] * (2 + QUAD + groups),
        scratch=[
            pltpu.VMEM(((PAIRED + EXTRA) * BLOCK, 64), F32),
            pltpu.VMEM(((depth + EXTRA) * BLOCK, 64), F32),
        ],
    )
    fms = [fm] + [far(fm, u) for u in range(1, groups)]
    alignment_gradient = call(
        align_kernel, sds(x.shape, BF16), [pg, mat, scale, hat, rstd]
    )
    pair_delta = call(
        pair_kernel,
        sds(adjoint.shape, BF16),
        pairs,
        scratch=[pltpu.VMEM((BLOCK * residues, 128), F32)],
    )
    merged = call(
        lambda *refs: merge_kernel(groups, *refs), sds((384, 128), BF16), w_quads + fms
    )
    merged = [merged] + [near(merged, t) for t in range(1, QUAD)]
    w, fma = call(final_kernel, [sds((1024, 128), F32), sds((256, 64), F32)], merged)
    return pair_delta, alignment_gradient, w, fma


def solution(mesh):
    devices = mesh.shape["row"]

    def body(*args):
        return on_device(devices, *args)

    return jax.shard_map(
        body,
        mesh=mesh,
        in_specs=(
            P("groups", "row", None),
            P(),
            P(),
            P(),
            P(),
            P(),
            P(),
            P(("groups", "row"), None, None),
            P("groups"),
            P("groups"),
        ),
        out_specs=(
            P(("groups", "row"), None, None),
            P("groups", "row", None),
            P("groups", None),
            P("groups", None),
        ),
        check_vma=False,
    )
```

```python
import jax
import jax.numpy as jnp
from jax import lax
from jax.experimental import pallas as pl
from jax.experimental.pallas import tpu as pltpu
from jax.sharding import PartitionSpec as P

PAIRED = 32
EXTRA = 8
QUAD = 4
BLOCK = 8
RANK = 32
PACKED = 80
F32 = jnp.float32
BF16 = jnp.bfloat16
SMEM = pl.BlockSpec(memory_space=pltpu.SMEM)


def vmem():
    return pl.BlockSpec(memory_space=pltpu.VMEM)


def params(mib=48):
    return pltpu.CompilerParams(vmem_limit_bytes=mib * 1024 * 1024)


def sds(shape, dtype):
    return jax.ShapeDtypeStruct(shape, dtype)


def place():
    k = lax.axis_index("row")
    return k >> 2, k & 3


def bounds_of(ref):
    ends, total = [], jnp.int32(0)
    for c in range(ref.shape[0]):
        total = total + ref[c]
        ends.append(total)
    return ends


def chain_of(residue, ends):
    chain = jnp.zeros(residue.shape, jnp.int32)
    for end in ends:
        chain = chain + jnp.where(residue >= end, 1, 0)
    return chain


def count_of(chain, hom_ref):
    picked = jnp.zeros(chain.shape, F32)
    for c in range(hom_ref.shape[0]):
        picked = jnp.where(chain == c, hom_ref[c].astype(F32), picked)
    return picked


def swap4(xs, low):
    lane = lax.broadcasted_iota(jnp.int32, xs[0].shape, 1)
    for bit, step in ((2, 2 * low), (1, low)):
        keep = (lane & step) == 0
        ys = list(xs)
        for q in range(4):
            if q & bit == 0:
                lo, hi = xs[q], xs[q | bit]
                ys[q] = jnp.where(keep, lo, pltpu.roll(hi, step, 1))
                ys[q | bit] = jnp.where(keep, pltpu.roll(lo, 128 - step, 1), hi)
        xs = ys
    return xs


def unpack(message):
    m = message.astype(F32)
    return [
        jnp.concatenate([m[0:32], m[64:72]], axis=0),
        jnp.concatenate([m[32:64], m[72:80]], axis=0),
    ]


def pack(lo, hi):
    return jnp.concatenate([lo[0:32], hi[0:32], lo[32:40], hi[32:40]], axis=0).astype(BF16)


def spread_rows(compact, chain, chains):
    rows = [compact[0:PAIRED]]
    extra = compact[PAIRED:]
    for c in range(chains):
        rows.append(jnp.where(chain == c, extra, 0.0))
    return jnp.concatenate(rows, axis=0)


def gather_rows(full, chain, chains):
    extra = jnp.zeros((EXTRA, full.shape[1]), F32)
    for c in range(chains):
        top = PAIRED + EXTRA * c
        extra = jnp.where(chain == c, full[top : top + EXTRA], extra)
    return jnp.concatenate([full[0:PAIRED], extra], axis=0)


def left_chain(a, b, ends):
    lane = lax.broadcasted_iota(jnp.int32, (EXTRA, 128), 1)
    residue = 32 * a + 8 * (b ^ (lane >> 5)) + (lane & 7)
    return jnp.concatenate([chain_of(residue, ends)] * 8, axis=1)


def right_chain(a, b, chunk, ends):
    lane = lax.broadcasted_iota(jnp.int32, (EXTRA, 256), 1)
    parts = []
    for tt in range(4):
        residue = 32 * (a ^ (4 * chunk + tt)) + 8 * b + (lane >> 5)
        parts.append(chain_of(residue, ends))
    return jnp.concatenate(parts, axis=1)


def spread_matrix():
    row = lax.broadcasted_iota(jnp.int32, (512, 512), 0)
    o = lax.broadcasted_iota(jnp.int32, (512, 512), 1)
    r, k = row >> 6, row & 63
    target = jnp.where(k < RANK, k * 8 + r, 256 + r * 32 + (k - RANK))
    return jnp.where(o == target, 1.0, 0.0).astype(BF16)


def swap_matrix():
    row = lax.broadcasted_iota(jnp.int32, (512, 512), 0)
    col = lax.broadcasted_iota(jnp.int32, (512, 512), 1)
    q, m = row >> 7, (row >> 3) & 3
    target = (m << 7) | (row & 0x67) | (q << 3)
    return jnp.where(col == target, 1.0, 0.0).astype(BF16)


def fetch(pairs, sems):
    copies = [pltpu.make_async_copy(a, b, sems.at[n]) for n, (a, b) in enumerate(pairs)]
    for c in copies:
        c.start()
    return copies


def start_kernel(
    x_hbm, adj_hbm, scale_hbm, shift_hbm, mat_hbm, off_hbm, len_hbm, hom_hbm, final_hbm,
    m0, m1, m2, m3, right_ref, norm_ref, hat_ref, rstd_ref, spread_ref, swap_ref, final_ref,
    x_ref, adj_ref, scale_ref, shift_ref, mat_ref, off_ref, len_ref, hom_ref,
    work, full, comp, sems,
):
    messages = (m0, m1, m2, m3)
    copies = fetch(
        [
            (adj_hbm, adj_ref), (x_hbm, x_ref), (scale_hbm, scale_ref),
            (shift_hbm, shift_ref), (mat_hbm, mat_ref), (off_hbm, off_ref),
            (len_hbm, len_ref), (hom_hbm, hom_ref), (final_hbm, final_ref),
        ],
        sems,
    )
    depth = x_ref.shape[0]
    residues = adj_ref.shape[1]
    groups = residues // 32
    chains = len_ref.shape[0]
    a, b = place()
    spread = spread_matrix()
    spread_ref[...] = spread
    swap_ref[...] = swap_matrix()
    copies[0].wait()
    work[...] = adj_ref[...].astype(F32).reshape(BLOCK * residues, 128)
    for t in range(QUAD):

        def step(u, _, t=t):
            tiles = []
            for jj in range(BLOCK):
                j = 32 * (a ^ u) + 8 * (b ^ t) + jj
                tiles.append(work[pl.ds(j, BLOCK, stride=residues), :])
            rows = pl.ds(pl.multiple_of(u * 64, 64), 64)
            messages[t][rows, :] = jnp.concatenate(tiles, axis=0).astype(BF16)
            return 0

        lax.fori_loop(0, groups, step, 0, unroll=groups <= 4)
    for c in copies[1:8]:
        c.wait()
    x = x_ref[...].astype(F32)
    centred = x - jnp.mean(x, axis=-1, keepdims=True)
    rstd = lax.rsqrt(jnp.mean(centred * centred, axis=-1, keepdims=True) + 1e-05)
    hat = (centred * rstd).reshape(depth * BLOCK, 256)
    normed = (hat * scale_ref[...] + shift_ref[...]).astype(BF16)
    hat_ref[...] = hat
    norm_ref[...] = normed
    rstd_ref[...] = jnp.broadcast_to(rstd, (depth, BLOCK, 128)).reshape(depth * BLOCK, 128)
    proj = lax.dot_general(
        normed, mat_ref[...], (((1,), (1,)), ((), ())), preferred_element_type=F32
    ) + off_ref[...]
    full[0 : depth * BLOCK, :] = proj
    full[depth * BLOCK :, :] = jnp.zeros((EXTRA * BLOCK, 64), F32)
    comp[0 : PAIRED * BLOCK, :] = proj[0 : PAIRED * BLOCK]
    residue = lax.broadcasted_iota(jnp.int32, (EXTRA * BLOCK, 64), 0)
    entry = residue >> 3
    chain = chain_of(32 * a + 8 * b + (residue & 7), bounds_of(len_ref))
    extra = jnp.zeros((EXTRA * BLOCK, 64), F32)
    start = jnp.int32(PAIRED)
    for c in range(chains):
        rows = full[pl.ds(pl.multiple_of(start * BLOCK, BLOCK), EXTRA * BLOCK), :]
        extra = jnp.where((chain == c) & (entry < hom_ref[c]), rows, extra)
        start = start + hom_ref[c]
    comp[PAIRED * BLOCK :, :] = extra
    rows = PAIRED + EXTRA
    wide = jnp.concatenate([comp[pl.ds(r, rows, stride=BLOCK), :] for r in range(BLOCK)], axis=1)
    out = jnp.dot(wide.astype(BF16), spread, preferred_element_type=F32)
    left = pack(out[:, 0:128], out[:, 128:256])
    for m in messages:
        m[groups * 64 :, :] = left
    right_ref[...] = pack(out[:, 256:384], out[:, 384:512])
    copies[8].wait()


def adjoint_kernel(
    chunks, len_ref, hom_ref, final_ref, swap_ref, m0, m1, m2, m3, s_ref, og_ref, ft_ref
):
    messages = (m0, m1, m2, m3)
    a, b = place()
    ends = bounds_of(len_ref)
    swap = swap_ref[...]
    low = lax.broadcasted_iota(jnp.int32, (32, 128), 0)
    chain_i, inv_same = [], []
    for t in range(QUAD):
        chain = chain_of(32 * a + 8 * (b ^ t) + (low & 7), ends)
        chain_i.append(chain)
        inv_same.append(1.0 / (float(PAIRED) + count_of(chain, hom_ref) + 0.001))
    inv_other = 1.0 / jnp.full((32, 128), PAIRED + 0.001, F32)
    final = final_ref[...]
    ft_ref[...] = final.astype(F32).T.astype(BF16)

    def step(g, _):
        blocks = []
        for tt in range(4):
            u = 4 * g + tt
            for half in range(2):
                chain_j = chain_of(32 * (a ^ u) + 8 * b + 4 * half + (low >> 3), ends)
                top = pl.ds(pl.multiple_of(u * 64 + half * 32, 32), 32)
                for t in range(QUAD):
                    inv = jnp.where(chain_i[t] == chain_j, inv_same[t], inv_other)
                    blocks.append(messages[t][top, :].astype(F32) * inv)
        s = jnp.concatenate(blocks, axis=0)
        s_ref[pl.ds(pl.multiple_of(g * 1024, 1024), 1024), :] = s.astype(BF16)
        st = s.T.astype(BF16)
        for cb in range(8):
            og = jnp.dot(
                final[cb * 128 : cb * 128 + 128, :], st, preferred_element_type=F32
            ).astype(BF16)
            wide = jnp.concatenate(
                [
                    jnp.concatenate(
                        [og[q * 32 : q * 32 + 32, jg * 128 : jg * 128 + 128] for q in range(4)],
                        axis=1,
                    )
                    for jg in range(8)
                ],
                axis=0,
            )
            moved = jnp.dot(wide, swap, preferred_element_type=F32).astype(BF16)
            for jg in range(8):
                for jl in range(4):
                    top = pl.ds(pl.multiple_of(g * 1024 + (jg * 4 + jl) * 32, 32), 32)
                    og_ref[top, cb * 128 : cb * 128 + 128] = moved[
                        jg * 32 : jg * 32 + 32, jl * 128 : jl * 128 + 128
                    ]
        return 0

    lax.fori_loop(0, chunks, step, 0, unroll=chunks == 1)


def left_lanes(lefts):
    parts = [unpack(m) for m in lefts]
    lanes = []
    for h in range(2):
        lanes += swap4([parts[t][h] for t in range(QUAD)], 32)
    return jnp.concatenate(lanes, axis=1)


def right_lanes(rights):
    return jnp.concatenate([blk for m in rights for blk in unpack(m)], axis=1)


def grad_kernel(
    chunks, len_ref, og_ref, m0, m1, m2, m3, r0, r1, r2, r3,
    l0, l1, l2, l3, g0, g1, g2, g3, lx_ref, rt_ref, lg_acc,
):
    messages, rights = (m0, m1, m2, m3), (r0, r1, r2, r3)
    lefts, grads = (l0, l1, l2, l3), (g0, g1, g2, g3)
    chains = len_ref.shape[0]
    a, b = place()
    ends = bounds_of(len_ref)
    chain_l = left_chain(a, b, ends)
    top = chunks * 256
    lx = spread_rows(
        left_lanes([m[top : top + PACKED, :] for m in messages]), chain_l, chains
    ).astype(BF16)
    lx_ref[...] = lx
    lg_acc[...] = jnp.zeros(lg_acc.shape, F32)

    def step(g, _):
        chain_r = right_chain(a, b, g, ends)
        at80 = pl.ds(pl.multiple_of(g * PACKED, 16), PACKED)
        at1024 = pl.ds(pl.multiple_of(g * 1024, 1024), 1024)
        rx = spread_rows(right_lanes([r[at80, :] for r in rights]), chain_r, chains)
        rt_ref[at1024, :] = rx.T.astype(BF16)
        og = og_ref[at1024, :]
        rg = lax.dot_general(lx, og, (((1,), (1,)), ((), ())), preferred_element_type=F32)
        rg = gather_rows(rg, chain_r, chains)
        for tt in range(4):
            grads[tt][at80, :] = pack(
                rg[:, tt * 256 : tt * 256 + 128], rg[:, tt * 256 + 128 : tt * 256 + 256]
            )
        lg_acc[...] += jnp.dot(rx.astype(BF16), og, preferred_element_type=F32)
        return 0

    lax.fori_loop(0, chunks, step, 0, unroll=chunks == 1)
    lgc = gather_rows(lg_acc[...], chain_l, chains)
    halves = []
    for h in range(2):
        xs = [lgc[:, (4 * h + q) * 128 : (4 * h + q + 1) * 128] for q in range(4)]
        halves.append(swap4(xs, 32))
    for t in range(QUAD):
        lefts[t][...] = pack(halves[0][t], halves[1][t])


def pair_kernel(
    chunks, len_ref, hom_ref, s_ref, ft_ref, swap_ref, bias_ref, lx_ref, rt_ref,
    l0, l1, l2, l3, own_ref, cross_ref, core_ref, p0, p1, px, n_buf, w_acc,
):
    lefts = (l0, l1, l2, l3)
    quads = ((own_ref, 0), (core_ref, 0), (cross_ref, 0), (core_ref, 256 + PACKED))
    pairs = ((p0, 0), (p1, 0), (px, 0), (px, chunks * 256))
    a, b = place()
    ends = bounds_of(len_ref)
    w_acc[...] = jnp.zeros(w_acc.shape, F32)
    lx = lx_ref[...]
    swap = swap_ref[...]
    bias = bias_ref[...]
    lane = lax.broadcasted_iota(jnp.int32, (8, 128), 1)
    chain_i = chain_of(32 * a + 8 * (b ^ (lane >> 5)) + (lane & 7), ends)
    same_inv = 1.0 / (float(PAIRED) + count_of(chain_i, hom_ref) + 0.001)
    other_inv = 1.0 / jnp.full((8, 128), PAIRED + 0.001, F32)

    def step(g, _):
        for jg in range(8):
            at = pl.ds(pl.multiple_of(g * 1024 + jg * 128, 128), 128)
            o = jnp.dot(rt_ref[at, :], lx, preferred_element_type=F32).astype(BF16)
            wide = jnp.concatenate(
                [
                    jnp.concatenate(
                        [o[q * 32 : q * 32 + 32, cb * 128 : cb * 128 + 128] for q in range(4)],
                        axis=1,
                    )
                    for cb in range(8)
                ],
                axis=0,
            )
            moved = jnp.dot(wide, swap, preferred_element_type=F32).astype(BF16)
            for cb in range(8):
                for cl in range(4):
                    row = (cb * 4 + cl) * 32
                    n_buf[row : row + 32, jg * 128 : jg * 128 + 128] = moved[
                        cb * 32 : cb * 32 + 32, cl * 128 : cl * 128 + 128
                    ]
        n = n_buf[...]
        s = s_ref[pl.ds(pl.multiple_of(g * 1024, 1024), 1024), :]
        w_acc[...] += jnp.dot(n, s, preferred_element_type=F32)
        pt = jnp.dot(ft_ref[...], n, preferred_element_type=F32)
        tiles = []
        for tt in range(4):
            for half in range(2):
                res_j = 32 * (a ^ (4 * g + tt)) + 8 * b + 4 * half + ((lane >> 3) & 3)
                inv = jnp.where(chain_i == chain_of(res_j, ends), same_inv, other_inv)
                inv_col = jnp.broadcast_to(inv[0:1], (128, 128)).T
                blk = tt * 2 + half
                tiles.append((pt[:, blk * 128 : blk * 128 + 128].T + bias) * inv_col)
        for t in range(QUAD):
            ref, top = pairs[t]
            ref[pl.ds(pl.multiple_of(top + g * 256, 256), 256), :] = jnp.concatenate(
                [v[t * 32 : t * 32 + 32] for v in tiles], axis=0
            ).astype(BF16)
        return 0

    lax.fori_loop(0, chunks, step, 0, unroll=chunks == 1)
    for t in range(QUAD):
        ref, top = quads[t]
        ref[top + 256 : top + 256 + PACKED, :] = lefts[t][...]
        rows = pl.ds(pl.multiple_of((b ^ t) * 256, 256), 256)
        ref[top : top + 256, :] = w_acc[rows, :].astype(BF16)


def total(values):
    out = values[0].astype(F32)
    for value in values[1:]:
        out = out + value.astype(F32)
    return out


def middle_kernel(own_ref, cross_ref, core_ref, mine_ref, theirs_ref):
    rows = 256 + PACKED
    mine_ref[...] = own_ref[...].astype(F32) + core_ref[0:rows, :].astype(F32)
    theirs_ref[...] = total([cross_ref[...], core_ref[rows:, :]]).astype(BF16)


def back_kernel(groups, len_ref, hom_ref, spread_ref, norm_ref, *refs):
    quads, rgs = refs[:2], refs[2 : 2 + groups]
    pg_ref, out_ref, comp, full = refs[2 + groups :]
    chains = len_ref.shape[0]
    depth8 = pg_ref.shape[0]
    a, b = place()
    out_ref[0:256, :] = total([q[0:256, :] for q in quads]).astype(BF16)
    lg = total([q[256:, :] for q in quads])
    rg = total([r[...] for r in rgs])
    wide = jnp.concatenate([blk for g in (lg, rg) for blk in unpack(g)], axis=1)
    rows = PAIRED + EXTRA
    per = lax.dot_general(
        wide.astype(BF16), spread_ref[...], (((1,), (1,)), ((), ())), preferred_element_type=F32
    )
    for r in range(BLOCK):
        comp[pl.ds(r, rows, stride=BLOCK), :] = per[:, r * 64 : r * 64 + 64]
    full[0 : PAIRED * BLOCK, :] = comp[0 : PAIRED * BLOCK, :]
    full[PAIRED * BLOCK :, :] = jnp.zeros((full.shape[0] - PAIRED * BLOCK, 64), F32)
    extra = comp[PAIRED * BLOCK :, :]
    residue = lax.broadcasted_iota(jnp.int32, (EXTRA * BLOCK, 64), 0)
    entry = residue >> 3
    chain = chain_of(32 * a + 8 * b + (residue & 7), bounds_of(len_ref))
    start = jnp.int32(PAIRED)
    for c in range(chains):
        at = pl.ds(pl.multiple_of(start * BLOCK, BLOCK), EXTRA * BLOCK)
        full[at, :] += jnp.where((chain == c) & (entry < hom_ref[c]), extra, 0.0)
        start = start + hom_ref[c]
    pg = full[0:depth8, :]
    pg_ref[...] = pg.astype(BF16)
    fm = jnp.dot(pg.T.astype(BF16), norm_ref[...], preferred_element_type=F32)
    out_ref[256:384, :] = jnp.concatenate([fm[:, 0:128], fm[:, 128:256]], axis=0).astype(BF16)


def align_kernel(pg_ref, mat_ref, scale_ref, hat_ref, rstd_ref, out_ref):
    g = jnp.dot(pg_ref[...], mat_ref[...], preferred_element_type=F32)
    g = g * scale_ref[...]
    hat = hat_ref[...]
    m1 = jnp.mean(g, axis=-1, keepdims=True)
    m2 = jnp.mean(g * hat, axis=-1, keepdims=True)
    rstd = rstd_ref[...]
    dx = (g - m1 - hat * m2) * jnp.concatenate([rstd, rstd], axis=1)
    out_ref[...] = dx.reshape(out_ref.shape).astype(BF16)


def assemble_kernel(*refs):
    pieces, out_ref, work = refs[:QUAD], refs[QUAD], refs[QUAD + 1]
    residues = out_ref.shape[1]
    groups = residues // 32
    tops = (0, 0, 0, groups * 64)
    a, b = place()
    for t in range(QUAD):

        def step(u, _, t=t):
            tile = pieces[t][pl.ds(pl.multiple_of(tops[t] + u * 64, 64), 64), :].astype(F32)
            for jj in range(BLOCK):
                j = 32 * (a ^ u) + 8 * (b ^ t) + jj
                work[pl.ds(j, BLOCK, stride=residues), :] = tile[jj * 8 : jj * 8 + 8]
            return 0

        lax.fori_loop(0, groups, step, 0, unroll=groups <= 4)
    out_ref[...] = work[...].reshape(out_ref.shape).astype(BF16)


def merge_kernel(*refs):
    refs[-1][...] = total([r[...] for r in refs[:-1]]).astype(BF16)


def relay_kernel(own_ref, cross_ref, out_ref):
    out_ref[0:256, :] = own_ref[0:256, :]
    out_ref[256:512, :] = cross_ref[0:256, :]
    out_ref[512:640, :] = total([own_ref[256:384, :], cross_ref[256:384, :]]).astype(BF16)


def final_kernel(mine_ref, core_ref, w_ref, fm_ref):
    _, b = place()
    for t in range(QUAD):
        rows = pl.ds(pl.multiple_of((b ^ t) * 256, 256), 256)
        ref, top = (mine_ref, core_ref)[t & 1], (t >> 1) * 256
        w_ref[rows, :] = ref[top : top + 256, :].astype(F32)
    fm = total([mine_ref[512:640, :], core_ref[512:640, :]])
    fm_ref[...] = jnp.concatenate([fm[0:64], fm[64:128]], axis=1)


HBM = pl.BlockSpec(memory_space=pltpu.HBM)


def call(kernel, outs, ins, in_specs=None, out_specs=None, scratch=(), work=0, mib=48):
    many = isinstance(outs, (list, tuple))
    if in_specs is not None:
        ins = [
            pltpu.with_memory_space_constraint(v, pltpu.HBM) if spec is HBM else v
            for v, spec in zip(ins, in_specs)
        ]
    return pl.pallas_call(
        kernel,
        out_shape=outs,
        in_specs=in_specs if in_specs is not None else [vmem()] * len(ins),
        out_specs=out_specs or ([vmem()] * len(outs) if many else vmem()),
        scratch_shapes=list(scratch),
        compiler_params=params(mib),
        cost_estimate=pl.CostEstimate(flops=work, bytes_accessed=work // 500, transcendentals=0),
    )(*ins)


def on_device(
    devices, x, scale, shift, mat, off, final, bias, adjoint, lengths, homologs
):
    groups = devices // QUAD
    chunks = groups // 4
    residues = adjoint.shape[1]
    depth = x.shape[0]
    scale, shift, off, bias = scale[None], shift[None], off[None], bias[None]
    mat = mat.T

    def near(value, t):
        return lax.ppermute(value, "row", [(k, k ^ t) for k in range(devices)])

    def far(value, u):
        return lax.ppermute(value, "row", [(k, k ^ (4 * u)) for k in range(devices)])

    def quad(parts):
        return [parts[0]] + [near(parts[t], t) for t in range(1, QUAD)]

    def by_slot(parts):
        if chunks == 1:
            return parts
        return [jnp.concatenate(parts[s::4], axis=0) for s in range(4)]

    def from_slot(parts, rows):
        if chunks == 1:
            return parts
        return [parts[u % 4][(u // 4) * rows : (u // 4 + 1) * rows] for u in range(groups)]

    *messages, right, normed, hat, rstd, spread, swap, final = call(
        start_kernel,
        [sds((groups * 64 + PACKED, 128), BF16)] * QUAD
        + [
            sds((PACKED, 128), BF16),
            sds((depth * BLOCK, 256), BF16),
            sds((depth * BLOCK, 256), F32),
            sds((depth * BLOCK, 128), F32),
            sds((512, 512), BF16),
            sds((512, 512), BF16),
            sds(final.shape, BF16),
        ],
        [x, adjoint, scale, shift, mat, off, lengths, homologs, final],
        in_specs=[HBM] * 9,
        scratch=[
            pltpu.VMEM(x.shape, BF16),
            pltpu.VMEM(adjoint.shape, BF16),
            pltpu.VMEM((1, 256), F32),
            pltpu.VMEM((1, 256), F32),
            pltpu.VMEM((64, 256), BF16),
            pltpu.VMEM((1, 64), F32),
            pltpu.SMEM(lengths.shape, jnp.int32),
            pltpu.SMEM(homologs.shape, jnp.int32),
            pltpu.VMEM((BLOCK * residues, 128), F32),
            pltpu.VMEM(((depth + EXTRA) * BLOCK, 64), F32),
            pltpu.VMEM(((PAIRED + EXTRA) * BLOCK, 64), F32),
            pltpu.SemaphoreType.DMA((9,)),
        ],
        work=10**9,
    )
    messages = quad(messages)
    rights = by_slot([right] + [far(right, u) for u in range(1, groups)])

    s, og, final_t = call(
        lambda *refs: adjoint_kernel(chunks, *refs),
        [
            sds((chunks * 1024, 128), BF16),
            sds((chunks * 1024, 1024), BF16),
            sds((128, 1024), BF16),
        ],
        [lengths, homologs, final, swap, *messages],
        in_specs=[SMEM] * 2 + [vmem()] * (2 + QUAD),
        work=2 * 10**9,
    )

    outs = call(
        lambda *refs: grad_kernel(chunks, *refs),
        [sds((PACKED, 128), BF16)] * QUAD
        + [sds((chunks * PACKED, 128), BF16)] * 4
        + [sds((128, 1024), BF16), sds((chunks * 1024, 128), BF16)],
        [lengths, og, *messages, *rights],
        in_specs=[SMEM] + [vmem()] * (1 + 2 * QUAD),
        scratch=[pltpu.VMEM((128, 1024), F32)],
        work=2 * 10**9,
    )
    lgs, rgs, (lx, rt) = outs[0:4], list(outs[4:8]), outs[8:10]
    rgs = from_slot(rgs, PACKED)
    rgs = [rgs[0]] + [far(rgs[u], u) for u in range(1, groups)]
    own, cross, core, pair_own, pair_core, pair_cross = call(
        lambda *refs: pair_kernel(chunks, *refs),
        [sds((256 + PACKED, 128), BF16)] * 2
        + [sds((512 + 2 * PACKED, 128), BF16)]
        + [sds((groups * 64, 128), BF16)] * 2
        + [sds((groups * 128, 128), BF16)],
        [lengths, homologs, s, final_t, swap, bias, lx, rt, *lgs],
        in_specs=[SMEM] * 2 + [vmem()] * (6 + QUAD),
        scratch=[pltpu.VMEM((1024, 1024), BF16), pltpu.VMEM((1024, 128), F32)],
        work=4 * 10**9,
    )
    core = near(core, 1)
    mine, theirs = call(
        middle_kernel,
        [sds((256 + PACKED, 128), F32), sds((256 + PACKED, 128), BF16)],
        [own, cross, core],
        work=10**7,
    )
    quads = [mine, near(theirs, 2)]

    pg, part = call(
        lambda *refs: back_kernel(groups, *refs),
        [sds((depth * BLOCK, 64), BF16), sds((384, 128), BF16)],
        [lengths, homologs, spread, normed, *quads, *rgs],
        in_specs=[SMEM] * 2 + [vmem()] * (4 + groups),
        scratch=[
            pltpu.VMEM(((PAIRED + EXTRA) * BLOCK, 64), F32),
            pltpu.VMEM(((depth + EXTRA) * BLOCK, 64), F32),
        ],
        work=10**9,
    )
    parts = [part] + [far(part, u) for u in range(1, groups)]
    pair_cross = near(pair_cross, 2)
    pairs = [pair_own, near(pair_core, 1), pair_cross, near(pair_cross, 1)]
    alignment_gradient = call(
        align_kernel,
        sds(x.shape, BF16),
        [pg, mat, scale, hat, rstd],
        work=10**9,
    )
    pair_delta = call(
        assemble_kernel,
        sds(adjoint.shape, BF16),
        pairs,
        scratch=[pltpu.VMEM((BLOCK * residues, 128), F32)],
        work=10**9,
    )
    parts, alignment_gradient, pair_delta = lax.optimization_barrier(
        (parts, alignment_gradient, pair_delta)
    )
    merged = call(merge_kernel, sds((384, 128), BF16), parts, work=10**7)
    relay = call(relay_kernel, sds((640, 128), BF16), [merged, near(merged, 2)], work=10**7)
    w, fm = call(
        final_kernel,
        [sds((1024, 128), F32), sds((64, 256), F32)],
        [relay, near(relay, 1)],
        work=10**8,
    )
    return pair_delta, alignment_gradient, w, fm.T


def solution(mesh):
    devices = mesh.shape["row"]

    def body(*args):
        return on_device(devices, *args)

    return jax.shard_map(
        body,
        mesh=mesh,
        in_specs=(
            P("groups", "row", None),
            P(),
            P(),
            P(),
            P(),
            P(),
            P(),
            P(("groups", "row"), None, None),
            P("groups"),
            P("groups"),
        ),
        out_specs=(
            P(("groups", "row"), None, None),
            P("groups", "row", None),
            P("groups", None),
            P("groups", None),
        ),
        check_vma=False,
    )
```

```python
import jax
import jax.numpy as jnp
from jax import lax
from jax.experimental import pallas as pl
from jax.experimental.pallas import tpu as pltpu
from jax.sharding import PartitionSpec as P

PAIRED = 32
EXTRA = 8
QUAD = 4
BLOCK = 8
RANK = 32
PACKED = 80
F32 = jnp.float32
BF16 = jnp.bfloat16
SMEM = pl.BlockSpec(memory_space=pltpu.SMEM)


def vmem():
    return pl.BlockSpec(memory_space=pltpu.VMEM)


def params(mib=48):
    return pltpu.CompilerParams(vmem_limit_bytes=mib * 1024 * 1024)


def sds(shape, dtype):
    return jax.ShapeDtypeStruct(shape, dtype)


def place():
    k = lax.axis_index("row")
    return k >> 2, k & 3


def bounds_of(ref):
    ends, total = [], jnp.int32(0)
    for c in range(ref.shape[0]):
        total = total + ref[c]
        ends.append(total)
    return ends


def chain_of(residue, ends):
    chain = jnp.zeros(residue.shape, jnp.int32)
    for end in ends:
        chain = chain + jnp.where(residue >= end, 1, 0)
    return chain


def count_of(chain, hom_ref):
    picked = jnp.zeros(chain.shape, F32)
    for c in range(hom_ref.shape[0]):
        picked = jnp.where(chain == c, hom_ref[c].astype(F32), picked)
    return picked


def swap4(xs, low):
    lane = lax.broadcasted_iota(jnp.int32, xs[0].shape, 1)
    for bit, step in ((2, 2 * low), (1, low)):
        keep = (lane & step) == 0
        ys = list(xs)
        for q in range(4):
            if q & bit == 0:
                lo, hi = xs[q], xs[q | bit]
                ys[q] = jnp.where(keep, lo, pltpu.roll(hi, step, 1))
                ys[q | bit] = jnp.where(keep, pltpu.roll(lo, 128 - step, 1), hi)
        xs = ys
    return xs


def unpack(message):
    m = message.astype(F32)
    return [
        jnp.concatenate([m[0:32], m[64:72]], axis=0),
        jnp.concatenate([m[32:64], m[72:80]], axis=0),
    ]


def pack(lo, hi):
    return jnp.concatenate([lo[0:32], hi[0:32], lo[32:40], hi[32:40]], axis=0).astype(BF16)


def spread_rows(compact, chain, chains):
    rows = [compact[0:PAIRED]]
    extra = compact[PAIRED:]
    for c in range(chains):
        rows.append(jnp.where(chain == c, extra, 0.0))
    return jnp.concatenate(rows, axis=0)


def gather_rows(full, chain, chains):
    extra = jnp.zeros((EXTRA, full.shape[1]), F32)
    for c in range(chains):
        top = PAIRED + EXTRA * c
        extra = jnp.where(chain == c, full[top : top + EXTRA], extra)
    return jnp.concatenate([full[0:PAIRED], extra], axis=0)


def left_chain(a, b, ends):
    lane = lax.broadcasted_iota(jnp.int32, (EXTRA, 128), 1)
    residue = 32 * a + 8 * (b ^ (lane >> 5)) + (lane & 7)
    return jnp.concatenate([chain_of(residue, ends)] * 8, axis=1)


def right_chain(a, b, chunk, ends):
    lane = lax.broadcasted_iota(jnp.int32, (EXTRA, 256), 1)
    parts = []
    for tt in range(4):
        residue = 32 * (a ^ (4 * chunk + tt)) + 8 * b + (lane >> 5)
        parts.append(chain_of(residue, ends))
    return jnp.concatenate(parts, axis=1)


def spread_matrix():
    row = lax.broadcasted_iota(jnp.int32, (512, 512), 0)
    o = lax.broadcasted_iota(jnp.int32, (512, 512), 1)
    r, k = row >> 6, row & 63
    target = jnp.where(k < RANK, k * 8 + r, 256 + r * 32 + (k - RANK))
    return jnp.where(o == target, 1.0, 0.0).astype(BF16)


def swap_matrix():
    row = lax.broadcasted_iota(jnp.int32, (512, 512), 0)
    col = lax.broadcasted_iota(jnp.int32, (512, 512), 1)
    q, m = row >> 7, (row >> 3) & 3
    target = (m << 7) | (row & 0x67) | (q << 3)
    return jnp.where(col == target, 1.0, 0.0).astype(BF16)


def swap_blocks(o, swap):
    blocks = o.shape[1] // 128
    wide = [
        jnp.concatenate(
            [
                o[(g * 4 + q) * 32 : (g * 4 + q + 1) * 32, blk * 128 : blk * 128 + 128]
                for q in range(4)
            ],
            axis=1,
        )
        for blk in range(blocks)
        for g in range(8)
    ]
    return jnp.dot(
        jnp.concatenate(wide, axis=0), swap, preferred_element_type=F32
    ).astype(BF16)


def fetch(pairs, sems):
    copies = [pltpu.make_async_copy(a, b, sems.at[n]) for n, (a, b) in enumerate(pairs)]
    for c in copies:
        c.start()
    return copies


def start_kernel(
    x_hbm, adj_hbm, scale_hbm, shift_hbm, mat_hbm, off_hbm, len_hbm, hom_hbm, final_hbm,
    m0, m1, m2, m3, right_ref, norm_ref, hat_ref, rstd_ref, spread_ref, swap_ref, final_ref,
    x_ref, adj_ref, scale_ref, shift_ref, mat_ref, off_ref, len_ref, hom_ref,
    work, full, comp, sems,
):
    messages = (m0, m1, m2, m3)
    copies = fetch(
        [
            (adj_hbm, adj_ref), (x_hbm, x_ref), (scale_hbm, scale_ref),
            (shift_hbm, shift_ref), (mat_hbm, mat_ref), (off_hbm, off_ref),
            (len_hbm, len_ref), (hom_hbm, hom_ref), (final_hbm, final_ref),
        ],
        sems,
    )
    depth = x_ref.shape[0]
    residues = adj_ref.shape[1]
    groups = residues // 32
    chains = len_ref.shape[0]
    a, b = place()
    spread = spread_matrix()
    spread_ref[...] = spread
    swap_ref[...] = swap_matrix()
    copies[0].wait()
    work[...] = adj_ref[...].astype(F32).reshape(BLOCK * residues, 128)
    for t in range(QUAD):

        def step(u, _, t=t):
            tiles = []
            for jj in range(BLOCK):
                j = 32 * (a ^ u) + 8 * (b ^ t) + jj
                tiles.append(work[pl.ds(j, BLOCK, stride=residues), :])
            rows = pl.ds(pl.multiple_of(u * 64, 64), 64)
            messages[t][rows, :] = jnp.concatenate(tiles, axis=0).astype(BF16)
            return 0

        lax.fori_loop(0, groups, step, 0, unroll=groups <= 4)
    for c in copies[1:8]:
        c.wait()
    x = x_ref[...].astype(F32)
    centred = x - jnp.mean(x, axis=-1, keepdims=True)
    rstd = lax.rsqrt(jnp.mean(centred * centred, axis=-1, keepdims=True) + 1e-05)
    hat = (centred * rstd).reshape(depth * BLOCK, 256)
    normed = (hat * scale_ref[...] + shift_ref[...]).astype(BF16)
    hat_ref[...] = hat
    norm_ref[...] = normed
    rstd_ref[...] = jnp.broadcast_to(rstd, (depth, BLOCK, 128)).reshape(depth * BLOCK, 128)
    proj = lax.dot_general(
        normed, mat_ref[...], (((1,), (1,)), ((), ())), preferred_element_type=F32
    ) + off_ref[...]
    full[0 : depth * BLOCK, :] = proj
    full[depth * BLOCK :, :] = jnp.zeros((EXTRA * BLOCK, 64), F32)
    comp[0 : PAIRED * BLOCK, :] = proj[0 : PAIRED * BLOCK]
    residue = lax.broadcasted_iota(jnp.int32, (EXTRA * BLOCK, 64), 0)
    entry = residue >> 3
    chain = chain_of(32 * a + 8 * b + (residue & 7), bounds_of(len_ref))
    extra = jnp.zeros((EXTRA * BLOCK, 64), F32)
    start = jnp.int32(PAIRED)
    for c in range(chains):
        rows = full[pl.ds(pl.multiple_of(start * BLOCK, BLOCK), EXTRA * BLOCK), :]
        extra = jnp.where((chain == c) & (entry < hom_ref[c]), rows, extra)
        start = start + hom_ref[c]
    comp[PAIRED * BLOCK :, :] = extra
    rows = PAIRED + EXTRA
    wide = jnp.concatenate([comp[pl.ds(r, rows, stride=BLOCK), :] for r in range(BLOCK)], axis=1)
    out = jnp.dot(wide.astype(BF16), spread, preferred_element_type=F32)
    left = pack(out[:, 0:128], out[:, 128:256])
    for m in messages:
        m[groups * 64 :, :] = left
    right_ref[...] = pack(out[:, 256:384], out[:, 384:512])
    copies[8].wait()


def adjoint_kernel(
    chunks, len_ref, hom_ref, final_ref, swap_ref, m0, m1, m2, m3,
    s_ref, og_ref, ft_ref, lx_ref,
):
    messages = (m0, m1, m2, m3)
    a, b = place()
    ends = bounds_of(len_ref)
    swap = swap_ref[...]
    bottom = chunks * 256
    lx_ref[...] = spread_rows(
        left_lanes([m[bottom : bottom + PACKED, :] for m in messages]),
        left_chain(a, b, ends),
        len_ref.shape[0],
    ).astype(BF16)
    low = lax.broadcasted_iota(jnp.int32, (32, 128), 0)
    chain_i, inv_same = [], []
    for t in range(QUAD):
        chain = chain_of(32 * a + 8 * (b ^ t) + (low & 7), ends)
        chain_i.append(chain)
        inv_same.append(1.0 / (float(PAIRED) + count_of(chain, hom_ref) + 0.001))
    inv_other = 1.0 / jnp.full((32, 128), PAIRED + 0.001, F32)
    final = final_ref[...]
    ft_ref[...] = final.astype(F32).T.astype(BF16)

    def step(g, _):
        blocks = []
        for tt in range(4):
            u = 4 * g + tt
            for half in range(2):
                chain_j = chain_of(32 * (a ^ u) + 8 * b + 4 * half + (low >> 3), ends)
                top = pl.ds(pl.multiple_of(u * 64 + half * 32, 32), 32)
                for t in range(QUAD):
                    inv = jnp.where(chain_i[t] == chain_j, inv_same[t], inv_other)
                    blocks.append(messages[t][top, :].astype(F32) * inv)
        s = jnp.concatenate(blocks, axis=0)
        s_ref[pl.ds(pl.multiple_of(g * 1024, 1024), 1024), :] = s.astype(BF16)
        st = s.T.astype(BF16)
        for half in range(2):
            og = jnp.dot(
                final, st[:, half * 512 : half * 512 + 512], preferred_element_type=F32
            ).astype(BF16)
            moved = swap_blocks(og, swap)
            for jg in range(4):
                for jl in range(4):
                    row = ((half * 4 + jg) * 4 + jl) * 32
                    at = pl.ds(pl.multiple_of(g * 1024 + row, 32), 32)
                    for cb in range(8):
                        top = (jg * 8 + cb) * 32
                        og_ref[at, cb * 128 : cb * 128 + 128] = moved[
                            top : top + 32, jl * 128 : jl * 128 + 128
                        ]
        return 0

    lax.fori_loop(0, chunks, step, 0, unroll=chunks == 1)


def left_lanes(lefts):
    parts = [unpack(m) for m in lefts]
    lanes = []
    for h in range(2):
        lanes += swap4([parts[t][h] for t in range(QUAD)], 32)
    return jnp.concatenate(lanes, axis=1)


def right_lanes(rights):
    return jnp.concatenate([blk for m in rights for blk in unpack(m)], axis=1)


def grad_kernel(
    chunks, len_ref, og_ref, lx_ref, r3, r2, r1, r0,
    l0, l1, l2, l3, g0, g1, g2, g3, rt_ref, lg_acc,
):
    rights = (r0, r1, r2, r3)
    lefts, grads = (l0, l1, l2, l3), (g0, g1, g2, g3)
    chains = len_ref.shape[0]
    a, b = place()
    ends = bounds_of(len_ref)
    chain_l = left_chain(a, b, ends)
    lx = lx_ref[...]
    lg_acc[...] = jnp.zeros(lg_acc.shape, F32)

    def step(g, _):
        chain_r = right_chain(a, b, g, ends)
        at80 = pl.ds(pl.multiple_of(g * PACKED, 16), PACKED)
        at1024 = pl.ds(pl.multiple_of(g * 1024, 1024), 1024)
        rx = spread_rows(right_lanes([r[at80, :] for r in rights]), chain_r, chains)
        rt_ref[at1024, :] = rx.T.astype(BF16)
        og = og_ref[at1024, :]
        rg = lax.dot_general(lx, og, (((1,), (1,)), ((), ())), preferred_element_type=F32)
        rg = gather_rows(rg, chain_r, chains)
        for tt in range(4):
            grads[tt][at80, :] = pack(
                rg[:, tt * 256 : tt * 256 + 128], rg[:, tt * 256 + 128 : tt * 256 + 256]
            )
        lg_acc[...] += jnp.dot(rx.astype(BF16), og, preferred_element_type=F32)
        return 0

    lax.fori_loop(0, chunks, step, 0, unroll=chunks == 1)
    lgc = gather_rows(lg_acc[...], chain_l, chains)
    halves = []
    for h in range(2):
        xs = [lgc[:, (4 * h + q) * 128 : (4 * h + q + 1) * 128] for q in range(4)]
        halves.append(swap4(xs, 32))
    for t in range(QUAD):
        lefts[t][...] = pack(halves[0][t], halves[1][t])


def pair_kernel(
    chunks, len_ref, hom_ref, s_ref, ft_ref, swap_ref, bias_ref, lx_ref, rt_ref,
    l0, l1, l2, l3, own_ref, cross_ref, core_ref, p0, p1, px, n_buf, w_acc,
):
    lefts = (l0, l1, l2, l3)
    quads = ((own_ref, 0), (core_ref, 0), (cross_ref, 0), (core_ref, 256 + PACKED))
    pairs = ((p0, 0), (p1, 0), (px, 0), (px, chunks * 256))
    a, b = place()
    ends = bounds_of(len_ref)
    w_acc[...] = jnp.zeros(w_acc.shape, F32)
    lx = lx_ref[...]
    swap = swap_ref[...]
    bias = bias_ref[...]
    lane = lax.broadcasted_iota(jnp.int32, (8, 128), 1)
    chain_i = chain_of(32 * a + 8 * (b ^ (lane >> 5)) + (lane & 7), ends)
    same_inv = 1.0 / (float(PAIRED) + count_of(chain_i, hom_ref) + 0.001)
    other_inv = 1.0 / jnp.full((8, 128), PAIRED + 0.001, F32)

    def step(g, _):
        rt = rt_ref[pl.ds(pl.multiple_of(g * 1024, 1024), 1024), :]
        for half in range(2):
            o = jnp.dot(
                rt, lx[:, half * 512 : half * 512 + 512], preferred_element_type=F32
            ).astype(BF16)
            moved = swap_blocks(o, swap)
            for cb in range(4):
                for cl in range(4):
                    row = ((half * 4 + cb) * 4 + cl) * 32
                    for jg in range(8):
                        top = (cb * 8 + jg) * 32
                        n_buf[row : row + 32, jg * 128 : jg * 128 + 128] = moved[
                            top : top + 32, cl * 128 : cl * 128 + 128
                        ]
        n = n_buf[...]
        s = s_ref[pl.ds(pl.multiple_of(g * 1024, 1024), 1024), :]
        w_acc[...] += jnp.dot(n, s, preferred_element_type=F32)
        pt = jnp.dot(ft_ref[...], n, preferred_element_type=F32)
        tiles = []
        for tt in range(4):
            for half in range(2):
                res_j = 32 * (a ^ (4 * g + tt)) + 8 * b + 4 * half + ((lane >> 3) & 3)
                inv = jnp.where(chain_i == chain_of(res_j, ends), same_inv, other_inv)
                inv_col = jnp.broadcast_to(inv[0:1], (128, 128)).T
                blk = tt * 2 + half
                tiles.append((pt[:, blk * 128 : blk * 128 + 128].T + bias) * inv_col)
        for t in range(QUAD):
            ref, top = pairs[t]
            ref[pl.ds(pl.multiple_of(top + g * 256, 256), 256), :] = jnp.concatenate(
                [v[t * 32 : t * 32 + 32] for v in tiles], axis=0
            ).astype(BF16)
        return 0

    lax.fori_loop(0, chunks, step, 0, unroll=chunks == 1)
    for t in range(QUAD):
        ref, top = quads[t]
        ref[top + 256 : top + 256 + PACKED, :] = lefts[t][...]
        rows = pl.ds(pl.multiple_of((b ^ t) * 256, 256), 256)
        ref[top : top + 256, :] = w_acc[rows, :].astype(BF16)


def total(values):
    out = values[0].astype(F32)
    for value in values[1:]:
        out = out + value.astype(F32)
    return out


def middle_kernel(own_ref, cross_ref, core_ref, mine_ref, theirs_ref):
    rows = 256 + PACKED
    mine_ref[...] = own_ref[...].astype(F32) + core_ref[0:rows, :].astype(F32)
    theirs_ref[...] = total([cross_ref[...], core_ref[rows:, :]]).astype(BF16)


def back_kernel(groups, len_ref, hom_ref, spread_ref, norm_ref, *refs):
    quads, rgs = refs[:2], refs[2 : 2 + groups]
    pg_ref, out_ref, comp, full = refs[2 + groups :]
    chains = len_ref.shape[0]
    depth8 = pg_ref.shape[0]
    a, b = place()
    lg = total([q[256:, :] for q in quads])
    rg = total([r[...] for r in rgs])
    wide = jnp.concatenate([blk for g in (lg, rg) for blk in unpack(g)], axis=1)
    rows = PAIRED + EXTRA
    per = lax.dot_general(
        wide.astype(BF16), spread_ref[...], (((1,), (1,)), ((), ())), preferred_element_type=F32
    )
    for r in range(BLOCK):
        comp[pl.ds(r, rows, stride=BLOCK), :] = per[:, r * 64 : r * 64 + 64]
    full[0 : PAIRED * BLOCK, :] = comp[0 : PAIRED * BLOCK, :]
    full[PAIRED * BLOCK :, :] = jnp.zeros((full.shape[0] - PAIRED * BLOCK, 64), F32)
    extra = comp[PAIRED * BLOCK :, :]
    residue = lax.broadcasted_iota(jnp.int32, (EXTRA * BLOCK, 64), 0)
    entry = residue >> 3
    chain = chain_of(32 * a + 8 * b + (residue & 7), bounds_of(len_ref))
    start = jnp.int32(PAIRED)
    for c in range(chains):
        at = pl.ds(pl.multiple_of(start * BLOCK, BLOCK), EXTRA * BLOCK)
        full[at, :] += jnp.where((chain == c) & (entry < hom_ref[c]), extra, 0.0)
        start = start + hom_ref[c]
    pg = full[0:depth8, :]
    pg_ref[...] = pg.astype(BF16)
    fm = jnp.dot(pg.T.astype(BF16), norm_ref[...], preferred_element_type=F32)
    out_ref[...] = jnp.concatenate([fm[:, 0:128], fm[:, 128:256]], axis=0).astype(BF16)


def fold_kernel(mine_ref, theirs_ref, out_ref):
    out_ref[...] = total([mine_ref[0:256, :], theirs_ref[0:256, :]]).astype(BF16)


def join_kernel(w0, w1, fm_ref, out_ref):
    out_ref[0:256, :] = total([w0[...], w1[...]]).astype(BF16)
    out_ref[256:384, :] = fm_ref[...]


def align_kernel(pg_ref, mat_ref, scale_ref, hat_ref, rstd_ref, out_ref):
    g = jnp.dot(pg_ref[...], mat_ref[...], preferred_element_type=F32)
    g = g * scale_ref[...]
    hat = hat_ref[...]
    m1 = jnp.mean(g, axis=-1, keepdims=True)
    m2 = jnp.mean(g * hat, axis=-1, keepdims=True)
    rstd = rstd_ref[...]
    dx = (g - m1 - hat * m2) * jnp.concatenate([rstd, rstd], axis=1)
    out_ref[...] = dx.reshape(out_ref.shape).astype(BF16)


def assemble_kernel(*refs):
    pieces, out_ref, work = refs[:QUAD], refs[QUAD], refs[QUAD + 1]
    residues = out_ref.shape[1]
    groups = residues // 32
    tops = (0, 0, 0, groups * 64)
    a, b = place()
    for t in range(QUAD):

        def step(u, _, t=t):
            tile = pieces[t][pl.ds(pl.multiple_of(tops[t] + u * 64, 64), 64), :].astype(F32)
            for jj in range(BLOCK):
                j = 32 * (a ^ u) + 8 * (b ^ t) + jj
                work[pl.ds(j, BLOCK, stride=residues), :] = tile[jj * 8 : jj * 8 + 8]
            return 0

        lax.fori_loop(0, groups, step, 0, unroll=groups <= 4)
    out_ref[...] = work[...].reshape(out_ref.shape).astype(BF16)


def merge_kernel(far_half, *refs):
    out_ref, fms = refs[-1], refs[:-1]
    out_ref[0:256, :] = total([fms[0][0:256, :], fms[far_half][0:256, :]]).astype(BF16)
    out_ref[256:384, :] = total([f[f.shape[0] - 128 :, :] for f in fms]).astype(BF16)


def relay_kernel(own_ref, cross_ref, out_ref):
    out_ref[0:256, :] = own_ref[0:256, :]
    out_ref[256:512, :] = cross_ref[0:256, :]
    out_ref[512:640, :] = total([own_ref[256:384, :], cross_ref[256:384, :]]).astype(BF16)


def final_kernel(mine_ref, core_ref, w_ref, fm_ref):
    _, b = place()
    for t in range(QUAD):
        rows = pl.ds(pl.multiple_of((b ^ t) * 256, 256), 256)
        ref, top = (mine_ref, core_ref)[t & 1], (t >> 1) * 256
        w_ref[rows, :] = ref[top : top + 256, :].astype(F32)
    fm = total([mine_ref[512:640, :], core_ref[512:640, :]])
    fm_ref[...] = jnp.concatenate([fm[0:64], fm[64:128]], axis=1)


HBM = pl.BlockSpec(memory_space=pltpu.HBM)


def call(kernel, outs, ins, in_specs=None, out_specs=None, scratch=(), work=0, mib=48):
    many = isinstance(outs, (list, tuple))
    if in_specs is not None:
        ins = [
            pltpu.with_memory_space_constraint(v, pltpu.HBM) if spec is HBM else v
            for v, spec in zip(ins, in_specs)
        ]
    return pl.pallas_call(
        kernel,
        out_shape=outs,
        in_specs=in_specs if in_specs is not None else [vmem()] * len(ins),
        out_specs=out_specs or ([vmem()] * len(outs) if many else vmem()),
        scratch_shapes=list(scratch),
        compiler_params=params(mib),
        cost_estimate=pl.CostEstimate(flops=work, bytes_accessed=work // 500, transcendentals=0),
    )(*ins)


def on_device(
    devices, x, scale, shift, mat, off, final, bias, adjoint, lengths, homologs
):
    groups = devices // QUAD
    chunks = groups // 4
    residues = adjoint.shape[1]
    depth = x.shape[0]
    scale, shift, off, bias = scale[None], shift[None], off[None], bias[None]
    mat = mat.T

    def near(value, t):
        return lax.ppermute(value, "row", [(k, k ^ t) for k in range(devices)])

    def far(value, u):
        return lax.ppermute(value, "row", [(k, k ^ (4 * u)) for k in range(devices)])

    def quad(parts):
        return [parts[0]] + [near(parts[t], t) for t in range(1, QUAD)]

    def by_slot(parts):
        if chunks == 1:
            return parts
        return [jnp.concatenate(parts[s::4], axis=0) for s in range(4)]

    def from_slot(parts, rows):
        if chunks == 1:
            return parts
        return [parts[u % 4][(u // 4) * rows : (u // 4 + 1) * rows] for u in range(groups)]

    *messages, right, normed, hat, rstd, spread, swap, final = call(
        start_kernel,
        [sds((groups * 64 + PACKED, 128), BF16)] * QUAD
        + [
            sds((PACKED, 128), BF16),
            sds((depth * BLOCK, 256), BF16),
            sds((depth * BLOCK, 256), F32),
            sds((depth * BLOCK, 128), F32),
            sds((512, 512), BF16),
            sds((512, 512), BF16),
            sds(final.shape, BF16),
        ],
        [x, adjoint, scale, shift, mat, off, lengths, homologs, final],
        in_specs=[HBM] * 9,
        scratch=[
            pltpu.VMEM(x.shape, BF16),
            pltpu.VMEM(adjoint.shape, BF16),
            pltpu.VMEM((1, 256), F32),
            pltpu.VMEM((1, 256), F32),
            pltpu.VMEM((64, 256), BF16),
            pltpu.VMEM((1, 64), F32),
            pltpu.SMEM(lengths.shape, jnp.int32),
            pltpu.SMEM(homologs.shape, jnp.int32),
            pltpu.VMEM((BLOCK * residues, 128), F32),
            pltpu.VMEM(((depth + EXTRA) * BLOCK, 64), F32),
            pltpu.VMEM(((PAIRED + EXTRA) * BLOCK, 64), F32),
            pltpu.SemaphoreType.DMA((9,)),
        ],
        work=10**9,
    )
    messages = quad(messages)
    rights = by_slot([right] + [far(right, u) for u in range(1, groups)])

    s, og, final_t, lx = call(
        lambda *refs: adjoint_kernel(chunks, *refs),
        [
            sds((chunks * 1024, 128), BF16),
            sds((chunks * 1024, 1024), BF16),
            sds((128, 1024), BF16),
            sds((128, 1024), BF16),
        ],
        [lengths, homologs, final, swap, *messages],
        in_specs=[SMEM] * 2 + [vmem()] * (2 + QUAD),
        work=2 * 10**9,
    )

    outs = call(
        lambda *refs: grad_kernel(chunks, *refs),
        [sds((PACKED, 128), BF16)] * QUAD
        + [sds((chunks * PACKED, 128), BF16)] * 4
        + [sds((chunks * 1024, 128), BF16)],
        [lengths, og, lx, *rights[::-1]],
        in_specs=[SMEM] + [vmem()] * (2 + QUAD),
        scratch=[pltpu.VMEM((128, 1024), F32)],
        work=2 * 10**9,
    )
    lgs, rgs, rt = outs[0:4], list(outs[4:8]), outs[8]
    rgs = from_slot(rgs, PACKED)
    rgs = [rgs[0]] + [far(rgs[u], u) for u in range(1, groups)]
    own, cross, core, pair_own, pair_core, pair_cross = call(
        lambda *refs: pair_kernel(chunks, *refs),
        [sds((256 + PACKED, 128), BF16)] * 2
        + [sds((512 + 2 * PACKED, 128), BF16)]
        + [sds((groups * 64, 128), BF16)] * 2
        + [sds((groups * 128, 128), BF16)],
        [lengths, homologs, s, final_t, swap, bias, lx, rt, *lgs],
        in_specs=[SMEM] * 2 + [vmem()] * (6 + QUAD),
        scratch=[pltpu.VMEM((1024, 1024), BF16), pltpu.VMEM((1024, 128), F32)],
        work=4 * 10**9,
    )
    core = near(core, 1)
    mine, theirs = call(
        middle_kernel,
        [sds((256 + PACKED, 128), F32), sds((256 + PACKED, 128), BF16)],
        [own, cross, core],
        work=10**7,
    )
    quads = [mine, near(theirs, 2)]

    pg, fm = call(
        lambda *refs: back_kernel(groups, *refs),
        [sds((depth * BLOCK, 64), BF16), sds((128, 128), BF16)],
        [lengths, homologs, spread, normed, *quads, *rgs],
        in_specs=[SMEM] * 2 + [vmem()] * (4 + groups),
        scratch=[
            pltpu.VMEM(((PAIRED + EXTRA) * BLOCK, 64), F32),
            pltpu.VMEM(((depth + EXTRA) * BLOCK, 64), F32),
        ],
        work=10**9,
    )
    half = groups // 2
    w = call(fold_kernel, sds((256, 128), BF16), quads, work=10**7)
    steps = [1 << k for k in range(half.bit_length() - 1)]
    for u in steps[:-1]:
        w = call(fold_kernel, sds((256, 128), BF16), [w, far(w, u)], work=10**7)
    part = call(join_kernel, sds((384, 128), BF16), [w, far(w, steps[-1]), fm], work=10**7)
    parts = [part] + [far(part if u == half else fm, u) for u in range(1, groups)]
    pair_cross = near(pair_cross, 2)
    pairs = [pair_own, near(pair_core, 1), pair_cross, near(pair_cross, 1)]
    alignment_gradient = call(
        align_kernel,
        sds(x.shape, BF16),
        [pg, mat, scale, hat, rstd],
        work=10**9,
    )
    pair_delta = call(
        assemble_kernel,
        sds(adjoint.shape, BF16),
        pairs,
        scratch=[pltpu.VMEM((BLOCK * residues, 128), F32)],
        work=10**9,
    )
    parts, alignment_gradient, pair_delta = lax.optimization_barrier(
        (parts, alignment_gradient, pair_delta)
    )
    merged = call(
        lambda *refs: merge_kernel(half, *refs), sds((384, 128), BF16), parts, work=10**7
    )
    relay = call(relay_kernel, sds((640, 128), BF16), [merged, near(merged, 2)], work=10**7)
    w, fm = call(
        final_kernel,
        [sds((1024, 128), F32), sds((64, 256), F32)],
        [relay, near(relay, 1)],
        work=10**8,
    )
    return pair_delta, alignment_gradient, w, fm.T


def solution(mesh):
    devices = mesh.shape["row"]

    def body(*args):
        return on_device(devices, *args)

    return jax.shard_map(
        body,
        mesh=mesh,
        in_specs=(
            P("groups", "row", None),
            P(),
            P(),
            P(),
            P(),
            P(),
            P(),
            P(("groups", "row"), None, None),
            P("groups"),
            P("groups"),
        ),
        out_specs=(
            P(("groups", "row"), None, None),
            P("groups", "row", None),
            P("groups", None),
            P("groups", None),
        ),
        check_vma=False,
    )
```

```python
import jax
import jax.numpy as jnp
from jax import lax
from jax.experimental import pallas as pl
from jax.experimental.pallas import tpu as pltpu
from jax.sharding import PartitionSpec as P

PAIRED = 32
EXTRA = 8
QUAD = 4
BLOCK = 8
RANK = 32
PACKED = 80
F32 = jnp.float32
BF16 = jnp.bfloat16
SMEM = pl.BlockSpec(memory_space=pltpu.SMEM)


def vmem():
    return pl.BlockSpec(memory_space=pltpu.VMEM)


def params(mib=48):
    return pltpu.CompilerParams(vmem_limit_bytes=mib * 1024 * 1024)


def sds(shape, dtype):
    return jax.ShapeDtypeStruct(shape, dtype)


def place():
    k = lax.axis_index("row")
    return k >> 2, k & 3


def bounds_of(ref):
    ends, total = [], jnp.int32(0)
    for c in range(ref.shape[0]):
        total = total + ref[c]
        ends.append(total)
    return ends


def chain_of(residue, ends):
    chain = jnp.zeros(residue.shape, jnp.int32)
    for end in ends:
        chain = chain + jnp.where(residue >= end, 1, 0)
    return chain


def count_of(chain, hom_ref):
    picked = jnp.zeros(chain.shape, F32)
    for c in range(hom_ref.shape[0]):
        picked = jnp.where(chain == c, hom_ref[c].astype(F32), picked)
    return picked


def swap4(xs, low):
    lane = lax.broadcasted_iota(jnp.int32, xs[0].shape, 1)
    for bit, step in ((2, 2 * low), (1, low)):
        keep = (lane & step) == 0
        ys = list(xs)
        for q in range(4):
            if q & bit == 0:
                lo, hi = xs[q], xs[q | bit]
                ys[q] = jnp.where(keep, lo, pltpu.roll(hi, step, 1))
                ys[q | bit] = jnp.where(keep, pltpu.roll(lo, 128 - step, 1), hi)
        xs = ys
    return xs


def unpack(message):
    m = message.astype(F32)
    return [
        jnp.concatenate([m[0:32], m[64:72]], axis=0),
        jnp.concatenate([m[32:64], m[72:80]], axis=0),
    ]


def pack(lo, hi):
    return jnp.concatenate([lo[0:32], hi[0:32], lo[32:40], hi[32:40]], axis=0).astype(BF16)


def spread_rows(compact, chain, chains):
    rows = [compact[0:PAIRED]]
    extra = compact[PAIRED:]
    for c in range(chains):
        rows.append(jnp.where(chain == c, extra, 0.0))
    return jnp.concatenate(rows, axis=0)


def gather_rows(full, chain, chains):
    extra = jnp.zeros((EXTRA, full.shape[1]), F32)
    for c in range(chains):
        top = PAIRED + EXTRA * c
        extra = jnp.where(chain == c, full[top : top + EXTRA], extra)
    return jnp.concatenate([full[0:PAIRED], extra], axis=0)


def left_chain(a, b, ends):
    lane = lax.broadcasted_iota(jnp.int32, (EXTRA, 128), 1)
    residue = 32 * a + 8 * (b ^ (lane >> 5)) + (lane & 7)
    return jnp.concatenate([chain_of(residue, ends)] * 8, axis=1)


def right_chain(a, b, chunk, ends):
    lane = lax.broadcasted_iota(jnp.int32, (EXTRA, 256), 1)
    parts = []
    for tt in range(4):
        residue = 32 * (a ^ (4 * chunk + tt)) + 8 * b + (lane >> 5)
        parts.append(chain_of(residue, ends))
    return jnp.concatenate(parts, axis=1)


def spread_matrix():
    row = lax.broadcasted_iota(jnp.int32, (512, 512), 0)
    o = lax.broadcasted_iota(jnp.int32, (512, 512), 1)
    r, k = row >> 6, row & 63
    target = jnp.where(k < RANK, k * 8 + r, 256 + r * 32 + (k - RANK))
    return jnp.where(o == target, 1.0, 0.0).astype(BF16)


def swap_matrix():
    row = lax.broadcasted_iota(jnp.int32, (512, 512), 0)
    col = lax.broadcasted_iota(jnp.int32, (512, 512), 1)
    q, m = row >> 7, (row >> 3) & 3
    target = (m << 7) | (row & 0x67) | (q << 3)
    return jnp.where(col == target, 1.0, 0.0).astype(BF16)


def swap_blocks(o, swap):
    blocks = o.shape[1] // 128
    wide = [
        jnp.concatenate(
            [
                o[(g * 4 + q) * 32 : (g * 4 + q + 1) * 32, blk * 128 : blk * 128 + 128]
                for q in range(4)
            ],
            axis=1,
        )
        for blk in range(blocks)
        for g in range(8)
    ]
    return jnp.dot(
        jnp.concatenate(wide, axis=0), swap, preferred_element_type=F32
    ).astype(BF16)


def fetch(pairs, sems):
    copies = [pltpu.make_async_copy(a, b, sems.at[n]) for n, (a, b) in enumerate(pairs)]
    for c in copies:
        c.start()
    return copies


def start_kernel(
    x_hbm, adj_hbm, scale_hbm, shift_hbm, mat_hbm, off_hbm, len_hbm, hom_hbm, final_hbm,
    m0, m1, m2, m3, right_ref, norm_ref, hat_ref, rstd_ref, spread_ref, swap_ref, final_ref,
    x_ref, adj_ref, scale_ref, shift_ref, mat_ref, off_ref, len_ref, hom_ref,
    work, full, comp, sems,
):
    messages = (m0, m1, m2, m3)
    copies = fetch(
        [
            (adj_hbm, adj_ref), (x_hbm, x_ref), (scale_hbm, scale_ref),
            (shift_hbm, shift_ref), (mat_hbm, mat_ref), (off_hbm, off_ref),
            (len_hbm, len_ref), (hom_hbm, hom_ref), (final_hbm, final_ref),
        ],
        sems,
    )
    depth = x_ref.shape[0]
    residues = adj_ref.shape[1]
    groups = residues // 32
    a, b = place()
    spread = spread_matrix()
    spread_ref[...] = spread
    swap_ref[...] = swap_matrix()
    copies[0].wait()
    work[...] = adj_ref[...].astype(F32).reshape(BLOCK * residues, 128)
    for t in range(QUAD):

        def step(u, _, t=t):
            tiles = []
            for jj in range(BLOCK):
                j = 32 * (a ^ u) + 8 * (b ^ t) + jj
                tiles.append(work[pl.ds(j, BLOCK, stride=residues), :])
            rows = pl.ds(pl.multiple_of(u * 64, 64), 64)
            messages[t][rows, :] = jnp.concatenate(tiles, axis=0).astype(BF16)
            return 0

        lax.fori_loop(0, groups, step, 0, unroll=groups <= 4)
    for c in copies[1:8]:
        c.wait()
    x = x_ref[...].astype(F32)
    centred = x - jnp.mean(x, axis=-1, keepdims=True)
    rstd = lax.rsqrt(jnp.mean(centred * centred, axis=-1, keepdims=True) + 1e-05)
    hat = (centred * rstd).reshape(depth * BLOCK, 256)
    normed = (hat * scale_ref[...] + shift_ref[...]).astype(BF16)
    hat_ref[...] = hat
    norm_ref[...] = normed
    rstd_ref[...] = jnp.broadcast_to(rstd, (depth, BLOCK, 128)).reshape(depth * BLOCK, 128)
    proj = lax.dot_general(
        normed, mat_ref[...], (((1,), (1,)), ((), ())), preferred_element_type=F32
    ) + off_ref[...]
    full[0 : depth * BLOCK, :] = proj
    full[depth * BLOCK :, :] = jnp.zeros((EXTRA * BLOCK, 64), F32)
    comp[0 : PAIRED * BLOCK, :] = proj[0 : PAIRED * BLOCK]
    comp[PAIRED * BLOCK :, :] = chain_rows(full, a, b, len_ref, hom_ref)
    rows = PAIRED + EXTRA
    wide = jnp.concatenate([comp[pl.ds(r, rows, stride=BLOCK), :] for r in range(BLOCK)], axis=1)
    out = jnp.dot(wide.astype(BF16), spread, preferred_element_type=F32)
    left = pack(out[:, 0:128], out[:, 128:256])
    for m in messages:
        m[groups * 64 :, :] = left
    right_ref[...] = pack(out[:, 256:384], out[:, 384:512])
    copies[8].wait()


def chain_rows(full, a, b, len_ref, hom_ref):
    lanes = full.shape[1]
    residue = lax.broadcasted_iota(jnp.int32, (EXTRA * BLOCK, lanes), 0)
    entry = residue >> 3
    chain = chain_of(32 * a + 8 * b + (residue & 7), bounds_of(len_ref))
    extra = jnp.zeros((EXTRA * BLOCK, lanes), F32)
    start = jnp.int32(PAIRED)
    for c in range(len_ref.shape[0]):
        rows = full[pl.ds(pl.multiple_of(start * BLOCK, BLOCK), EXTRA * BLOCK), :]
        extra = jnp.where((chain == c) & (entry < hom_ref[c]), rows, extra)
        start = start + hom_ref[c]
    return extra


def adjoint_kernel(
    chunks, len_ref, hom_ref, final_ref, swap_ref, spread_ref, norm_ref, m0, m1, m2, m3,
    s_ref, og_ref, ft_ref, lx_ref, lt_ref, gather_ref, few_ref, nfull,
):
    messages = (m0, m1, m2, m3)
    a, b = place()
    ends = bounds_of(len_ref)
    swap = swap_ref[...]
    bottom = chunks * 256
    lx = spread_rows(
        left_lanes([m[bottom : bottom + PACKED, :] for m in messages]),
        left_chain(a, b, ends),
        len_ref.shape[0],
    )
    lx_ref[...] = lx.astype(BF16)
    lt_ref[...] = lx.T.astype(BF16)
    gather_ref[...] = spread_ref[...].astype(F32).T.astype(BF16)
    depth8 = norm_ref.shape[0]
    nfull[0:depth8, :] = norm_ref[...].astype(F32)
    nfull[depth8:, :] = jnp.zeros((EXTRA * BLOCK, 256), F32)
    few_ref[0 : PAIRED * BLOCK, :] = norm_ref[0 : PAIRED * BLOCK, :]
    few_ref[PAIRED * BLOCK :, :] = chain_rows(nfull, a, b, len_ref, hom_ref).astype(BF16)
    low = lax.broadcasted_iota(jnp.int32, (32, 128), 0)
    chain_i, inv_same = [], []
    for t in range(QUAD):
        chain = chain_of(32 * a + 8 * (b ^ t) + (low & 7), ends)
        chain_i.append(chain)
        inv_same.append(1.0 / (float(PAIRED) + count_of(chain, hom_ref) + 0.001))
    inv_other = 1.0 / jnp.full((32, 128), PAIRED + 0.001, F32)
    final = final_ref[...]
    ft_ref[...] = final.astype(F32).T.astype(BF16)

    def step(g, _):
        blocks = []
        for tt in range(4):
            u = 4 * g + tt
            for half in range(2):
                chain_j = chain_of(32 * (a ^ u) + 8 * b + 4 * half + (low >> 3), ends)
                top = pl.ds(pl.multiple_of(u * 64 + half * 32, 32), 32)
                for t in range(QUAD):
                    inv = jnp.where(chain_i[t] == chain_j, inv_same[t], inv_other)
                    blocks.append(messages[t][top, :].astype(F32) * inv)
        s = jnp.concatenate(blocks, axis=0)
        s_ref[pl.ds(pl.multiple_of(g * 1024, 1024), 1024), :] = s.astype(BF16)
        st = s.T.astype(BF16)
        for half in range(2):
            og = jnp.dot(
                final, st[:, half * 512 : half * 512 + 512], preferred_element_type=F32
            ).astype(BF16)
            moved = swap_blocks(og, swap)
            for jg in range(4):
                for jl in range(4):
                    row = ((half * 4 + jg) * 4 + jl) * 32
                    at = pl.ds(pl.multiple_of(g * 1024 + row, 32), 32)
                    for cb in range(8):
                        top = (jg * 8 + cb) * 32
                        og_ref[at, cb * 128 : cb * 128 + 128] = moved[
                            top : top + 32, jl * 128 : jl * 128 + 128
                        ]
        return 0

    lax.fori_loop(0, chunks, step, 0, unroll=chunks == 1)


def left_lanes(lefts):
    parts = [unpack(m) for m in lefts]
    lanes = []
    for h in range(2):
        lanes += swap4([parts[t][h] for t in range(QUAD)], 32)
    return jnp.concatenate(lanes, axis=1)


def right_lanes(rights):
    return jnp.concatenate([blk for m in rights for blk in unpack(m)], axis=1)


def grad_kernel(
    chunks, len_ref, og_ref, lt_ref, r3, r2, r1, r0,
    l0, l1, l2, l3, g0, g1, g2, g3, rt_ref, lg_acc,
):
    rights = (r0, r1, r2, r3)
    lefts, grads = (l0, l1, l2, l3), (g0, g1, g2, g3)
    chains = len_ref.shape[0]
    a, b = place()
    ends = bounds_of(len_ref)
    chain_l = left_chain(a, b, ends)
    lt = lt_ref[...]
    lg_acc[...] = jnp.zeros(lg_acc.shape, F32)

    def step(g, _):
        chain_r = right_chain(a, b, g, ends)
        at80 = pl.ds(pl.multiple_of(g * PACKED, 16), PACKED)
        at1024 = pl.ds(pl.multiple_of(g * 1024, 1024), 1024)
        rx = spread_rows(right_lanes([r[at80, :] for r in rights]), chain_r, chains)
        rt_ref[at1024, :] = rx.T.astype(BF16)
        og = og_ref[at1024, :]
        rg = jnp.dot(og, lt, preferred_element_type=F32).T
        rg = gather_rows(rg, chain_r, chains)
        for tt in range(4):
            grads[tt][at80, :] = pack(
                rg[:, tt * 256 : tt * 256 + 128], rg[:, tt * 256 + 128 : tt * 256 + 256]
            )
        lg_acc[...] += jnp.dot(rx.astype(BF16), og, preferred_element_type=F32)
        return 0

    lax.fori_loop(0, chunks, step, 0, unroll=chunks == 1)
    lgc = gather_rows(lg_acc[...], chain_l, chains)
    halves = []
    for h in range(2):
        xs = [lgc[:, (4 * h + q) * 128 : (4 * h + q + 1) * 128] for q in range(4)]
        halves.append(swap4(xs, 32))
    for t in range(QUAD):
        lefts[t][...] = pack(halves[0][t], halves[1][t])


def pair_kernel(
    chunks, len_ref, hom_ref, s_ref, ft_ref, swap_ref, bias_ref, lx_ref, rt_ref,
    l0, l1, l2, l3, own_ref, cross_ref, core_ref, p0, p1, px, n_buf, w_acc,
):
    lefts = (l0, l1, l2, l3)
    quads = ((own_ref, 0), (core_ref, 0), (cross_ref, 0), (core_ref, 256 + PACKED))
    pairs = ((p0, 0), (p1, 0), (px, 0), (px, chunks * 256))
    a, b = place()
    ends = bounds_of(len_ref)
    w_acc[...] = jnp.zeros(w_acc.shape, F32)
    lx = lx_ref[...]
    swap = swap_ref[...]
    bias = bias_ref[...]
    lane = lax.broadcasted_iota(jnp.int32, (8, 128), 1)
    chain_i = chain_of(32 * a + 8 * (b ^ (lane >> 5)) + (lane & 7), ends)
    same_inv = 1.0 / (float(PAIRED) + count_of(chain_i, hom_ref) + 0.001)
    other_inv = 1.0 / jnp.full((8, 128), PAIRED + 0.001, F32)

    def step(g, _):
        rt = rt_ref[pl.ds(pl.multiple_of(g * 1024, 1024), 1024), :]
        for half in range(2):
            o = jnp.dot(
                rt, lx[:, half * 512 : half * 512 + 512], preferred_element_type=F32
            ).astype(BF16)
            moved = swap_blocks(o, swap)
            for cb in range(4):
                for cl in range(4):
                    row = ((half * 4 + cb) * 4 + cl) * 32
                    for jg in range(8):
                        top = (cb * 8 + jg) * 32
                        n_buf[row : row + 32, jg * 128 : jg * 128 + 128] = moved[
                            top : top + 32, cl * 128 : cl * 128 + 128
                        ]
        n = n_buf[...]
        s = s_ref[pl.ds(pl.multiple_of(g * 1024, 1024), 1024), :]
        w_acc[...] += jnp.dot(n, s, preferred_element_type=F32)
        pt = jnp.dot(ft_ref[...], n, preferred_element_type=F32)
        tiles = []
        for tt in range(4):
            for half in range(2):
                res_j = 32 * (a ^ (4 * g + tt)) + 8 * b + 4 * half + ((lane >> 3) & 3)
                inv = jnp.where(chain_i == chain_of(res_j, ends), same_inv, other_inv)
                inv_col = jnp.broadcast_to(inv[0:1], (128, 128)).T
                blk = tt * 2 + half
                tiles.append((pt[:, blk * 128 : blk * 128 + 128].T + bias) * inv_col)
        for t in range(QUAD):
            ref, top = pairs[t]
            ref[pl.ds(pl.multiple_of(top + g * 256, 256), 256), :] = jnp.concatenate(
                [v[t * 32 : t * 32 + 32] for v in tiles], axis=0
            ).astype(BF16)
        return 0

    lax.fori_loop(0, chunks, step, 0, unroll=chunks == 1)
    for t in range(QUAD):
        ref, top = quads[t]
        ref[top + 256 : top + 256 + PACKED, :] = lefts[t][...]
        rows = pl.ds(pl.multiple_of((b ^ t) * 256, 256), 256)
        ref[top : top + 256, :] = w_acc[rows, :].astype(BF16)


def total(values):
    out = values[0].astype(F32)
    for value in values[1:]:
        out = out + value.astype(F32)
    return out


def middle_kernel(own_ref, cross_ref, core_ref, mine_ref, theirs_ref):
    rows = 256 + PACKED
    mine_ref[...] = own_ref[...].astype(F32) + core_ref[0:rows, :].astype(F32)
    theirs_ref[...] = total([cross_ref[...], core_ref[rows:, :]]).astype(BF16)


def back_kernel(groups, gather_ref, few_ref, *refs):
    quads, rgs = refs[:2], refs[2 : 2 + groups]
    pg_ref, out_ref, comp = refs[2 + groups :]
    lg = total([q[256:, :] for q in quads])
    rg = total([r[...] for r in rgs])
    wide = jnp.concatenate([blk for g in (lg, rg) for blk in unpack(g)], axis=1)
    rows = PAIRED + EXTRA
    per = jnp.dot(wide.astype(BF16), gather_ref[...], preferred_element_type=F32)
    for r in range(BLOCK):
        comp[pl.ds(r, rows, stride=BLOCK), :] = per[:, r * 64 : r * 64 + 64]
    pg = comp[...]
    pg_ref[...] = pg.astype(BF16)
    fm = jnp.dot(pg.T.astype(BF16), few_ref[...], preferred_element_type=F32)
    out_ref[...] = jnp.concatenate([fm[:, 0:128], fm[:, 128:256]], axis=0).astype(BF16)


def fold_kernel(mine_ref, theirs_ref, out_ref):
    out_ref[...] = total([mine_ref[0:256, :], theirs_ref[0:256, :]]).astype(BF16)


def join_kernel(w0, w1, fm_ref, out_ref):
    out_ref[0:256, :] = total([w0[...], w1[...]]).astype(BF16)
    out_ref[256:384, :] = fm_ref[...]


def align_kernel(
    len_ref, hom_ref, pg_ref, mat_ref, scale_ref, hat_ref, rstd_ref, out_ref, full
):
    a, b = place()
    depth8 = hat_ref.shape[0]
    full[0 : PAIRED * BLOCK, :] = pg_ref[0 : PAIRED * BLOCK, :].astype(F32)
    full[PAIRED * BLOCK :, :] = jnp.zeros((full.shape[0] - PAIRED * BLOCK, 64), F32)
    extra = pg_ref[PAIRED * BLOCK :, :].astype(F32)
    residue = lax.broadcasted_iota(jnp.int32, (EXTRA * BLOCK, 64), 0)
    entry = residue >> 3
    chain = chain_of(32 * a + 8 * b + (residue & 7), bounds_of(len_ref))
    start = jnp.int32(PAIRED)
    for c in range(len_ref.shape[0]):
        at = pl.ds(pl.multiple_of(start * BLOCK, BLOCK), EXTRA * BLOCK)
        full[at, :] += jnp.where((chain == c) & (entry < hom_ref[c]), extra, 0.0)
        start = start + hom_ref[c]
    g = jnp.dot(full[0:depth8, :].astype(BF16), mat_ref[...], preferred_element_type=F32)
    g = g * scale_ref[...]
    hat = hat_ref[...]
    m1 = jnp.mean(g, axis=-1, keepdims=True)
    m2 = jnp.mean(g * hat, axis=-1, keepdims=True)
    rstd = rstd_ref[...]
    dx = (g - m1 - hat * m2) * jnp.concatenate([rstd, rstd], axis=1)
    out_ref[...] = dx.reshape(out_ref.shape).astype(BF16)


def assemble_kernel(*refs):
    pieces, out_ref, work = refs[:QUAD], refs[QUAD], refs[QUAD + 1]
    residues = out_ref.shape[1]
    groups = residues // 32
    tops = (0, 0, 0, groups * 64)
    a, b = place()
    for t in range(QUAD):

        def step(u, _, t=t):
            tile = pieces[t][pl.ds(pl.multiple_of(tops[t] + u * 64, 64), 64), :].astype(F32)
            for jj in range(BLOCK):
                j = 32 * (a ^ u) + 8 * (b ^ t) + jj
                work[pl.ds(j, BLOCK, stride=residues), :] = tile[jj * 8 : jj * 8 + 8]
            return 0

        lax.fori_loop(0, groups, step, 0, unroll=groups <= 4)
    out_ref[...] = work[...].reshape(out_ref.shape).astype(BF16)


def merge_kernel(*refs):
    out_ref, fms = refs[-1], refs[:-1]
    out_ref[0:256, :] = total([fms[0][0:256, :], fms[1][0:256, :]]).astype(BF16)
    out_ref[256:384, :] = total([f[f.shape[0] - 128 :, :] for f in fms]).astype(BF16)


def relay_kernel(own_ref, cross_ref, out_ref):
    out_ref[0:256, :] = own_ref[0:256, :]
    out_ref[256:512, :] = cross_ref[0:256, :]
    out_ref[512:640, :] = total([own_ref[256:384, :], cross_ref[256:384, :]]).astype(BF16)


def final_kernel(mine_ref, core_ref, w_ref, fm_ref):
    _, b = place()
    for t in range(QUAD):
        rows = pl.ds(pl.multiple_of((b ^ t) * 256, 256), 256)
        ref, top = (mine_ref, core_ref)[t & 1], (t >> 1) * 256
        w_ref[rows, :] = ref[top : top + 256, :].astype(F32)
    fm = total([mine_ref[512:640, :], core_ref[512:640, :]])
    fm_ref[...] = jnp.concatenate([fm[0:64], fm[64:128]], axis=1)


HBM = pl.BlockSpec(memory_space=pltpu.HBM)


def call(kernel, outs, ins, in_specs=None, out_specs=None, scratch=(), work=0, mib=48):
    many = isinstance(outs, (list, tuple))
    if in_specs is not None:
        ins = [
            pltpu.with_memory_space_constraint(v, pltpu.HBM) if spec is HBM else v
            for v, spec in zip(ins, in_specs)
        ]
    return pl.pallas_call(
        kernel,
        out_shape=outs,
        in_specs=in_specs if in_specs is not None else [vmem()] * len(ins),
        out_specs=out_specs or ([vmem()] * len(outs) if many else vmem()),
        scratch_shapes=list(scratch),
        compiler_params=params(mib),
        cost_estimate=pl.CostEstimate(flops=work, bytes_accessed=work // 500, transcendentals=0),
    )(*ins)


def on_device(
    devices, x, scale, shift, mat, off, final, bias, adjoint, lengths, homologs
):
    groups = devices // QUAD
    chunks = groups // 4
    residues = adjoint.shape[1]
    depth = x.shape[0]
    scale, shift, off, bias = scale[None], shift[None], off[None], bias[None]
    mat = mat.T

    def near(value, t):
        return lax.ppermute(value, "row", [(k, k ^ t) for k in range(devices)])

    def far(value, u):
        return lax.ppermute(value, "row", [(k, k ^ (4 * u)) for k in range(devices)])

    def quad(parts):
        return [parts[0]] + [near(parts[t], t) for t in range(1, QUAD)]

    def by_slot(parts):
        if chunks == 1:
            return parts
        return [jnp.concatenate(parts[s::4], axis=0) for s in range(4)]

    def from_slot(parts, rows):
        if chunks == 1:
            return parts
        return [parts[u % 4][(u // 4) * rows : (u // 4 + 1) * rows] for u in range(groups)]

    *messages, right, normed, hat, rstd, spread, swap, final = call(
        start_kernel,
        [sds((groups * 64 + PACKED, 128), BF16)] * QUAD
        + [
            sds((PACKED, 128), BF16),
            sds((depth * BLOCK, 256), BF16),
            sds((depth * BLOCK, 256), F32),
            sds((depth * BLOCK, 128), F32),
            sds((512, 512), BF16),
            sds((512, 512), BF16),
            sds(final.shape, BF16),
        ],
        [x, adjoint, scale, shift, mat, off, lengths, homologs, final],
        in_specs=[HBM] * 9,
        scratch=[
            pltpu.VMEM(x.shape, BF16),
            pltpu.VMEM(adjoint.shape, BF16),
            pltpu.VMEM((1, 256), F32),
            pltpu.VMEM((1, 256), F32),
            pltpu.VMEM((64, 256), BF16),
            pltpu.VMEM((1, 64), F32),
            pltpu.SMEM(lengths.shape, jnp.int32),
            pltpu.SMEM(homologs.shape, jnp.int32),
            pltpu.VMEM((BLOCK * residues, 128), F32),
            pltpu.VMEM(((depth + EXTRA) * BLOCK, 64), F32),
            pltpu.VMEM(((PAIRED + EXTRA) * BLOCK, 64), F32),
            pltpu.SemaphoreType.DMA((9,)),
        ],
        work=10**9,
    )
    messages = quad(messages)
    rights = by_slot([right] + [far(right, u) for u in range(1, groups)])

    s, og, final_t, lx, lt, gather, few = call(
        lambda *refs: adjoint_kernel(chunks, *refs),
        [
            sds((chunks * 1024, 128), BF16),
            sds((chunks * 1024, 1024), BF16),
            sds((128, 1024), BF16),
            sds((128, 1024), BF16),
            sds((1024, 128), BF16),
            sds((512, 512), BF16),
            sds(((PAIRED + EXTRA) * BLOCK, 256), BF16),
        ],
        [lengths, homologs, final, swap, spread, normed, *messages],
        in_specs=[SMEM] * 2 + [vmem()] * (4 + QUAD),
        scratch=[pltpu.VMEM(((depth + EXTRA) * BLOCK, 256), F32)],
        work=2 * 10**9,
    )

    outs = call(
        lambda *refs: grad_kernel(chunks, *refs),
        [sds((PACKED, 128), BF16)] * QUAD
        + [sds((chunks * PACKED, 128), BF16)] * 4
        + [sds((chunks * 1024, 128), BF16)],
        [lengths, og, lt, *rights[::-1]],
        in_specs=[SMEM] + [vmem()] * (2 + QUAD),
        scratch=[pltpu.VMEM((128, 1024), F32)],
        work=2 * 10**9,
    )
    lgs, rgs, rt = outs[0:4], list(outs[4:8]), outs[8]
    rgs = from_slot(rgs, PACKED)
    rgs = [rgs[0]] + [far(rgs[u], u) for u in range(1, groups)]
    own, cross, core, pair_own, pair_core, pair_cross = call(
        lambda *refs: pair_kernel(chunks, *refs),
        [sds((256 + PACKED, 128), BF16)] * 2
        + [sds((512 + 2 * PACKED, 128), BF16)]
        + [sds((groups * 64, 128), BF16)] * 2
        + [sds((groups * 128, 128), BF16)],
        [lengths, homologs, s, final_t, swap, bias, lx, rt, *lgs],
        in_specs=[SMEM] * 2 + [vmem()] * (6 + QUAD),
        scratch=[pltpu.VMEM((1024, 1024), BF16), pltpu.VMEM((1024, 128), F32)],
        work=4 * 10**9,
    )
    core = near(core, 1)
    mine, theirs = call(
        middle_kernel,
        [sds((256 + PACKED, 128), F32), sds((256 + PACKED, 128), BF16)],
        [own, cross, core],
        work=10**7,
    )
    quads = [mine, near(theirs, 2)]

    pg, fm = call(
        lambda *refs: back_kernel(groups, *refs),
        [sds(((PAIRED + EXTRA) * BLOCK, 64), BF16), sds((128, 128), BF16)],
        [gather, few, *quads, *rgs],
        scratch=[pltpu.VMEM(((PAIRED + EXTRA) * BLOCK, 64), F32)],
        work=10**9,
    )
    half = groups // 2
    w = call(fold_kernel, sds((256, 128), BF16), quads, work=10**7)
    steps = [half >> k for k in range(half.bit_length() - 1)]
    for u in steps[:-1]:
        w = call(fold_kernel, sds((256, 128), BF16), [w, far(w, u)], work=10**7)
    part = call(join_kernel, sds((384, 128), BF16), [w, far(w, steps[-1]), fm], work=10**7)
    parts = [part] + [far(part if u == 1 else fm, u) for u in range(1, groups)]
    pair_cross = near(pair_cross, 2)
    pairs = [pair_own, near(pair_core, 1), pair_cross, near(pair_cross, 1)]
    alignment_gradient = call(
        align_kernel,
        sds(x.shape, BF16),
        [lengths, homologs, pg, mat, scale, hat, rstd],
        in_specs=[SMEM] * 2 + [vmem()] * 5,
        scratch=[pltpu.VMEM(((depth + EXTRA) * BLOCK, 64), F32)],
        work=10**9,
    )
    pair_delta = call(
        assemble_kernel,
        sds(adjoint.shape, BF16),
        pairs,
        scratch=[pltpu.VMEM((BLOCK * residues, 128), F32)],
        work=10**9,
    )
    parts, alignment_gradient, pair_delta = lax.optimization_barrier(
        (parts, alignment_gradient, pair_delta)
    )
    merged = call(
        merge_kernel, sds((384, 128), BF16), parts, work=10**7
    )
    relay = call(relay_kernel, sds((640, 128), BF16), [merged, near(merged, 2)], work=10**7)
    w, fm = call(
        final_kernel,
        [sds((1024, 128), F32), sds((64, 256), F32)],
        [relay, near(relay, 1)],
        work=10**8,
    )
    return pair_delta, alignment_gradient, w, fm.T


def solution(mesh):
    devices = mesh.shape["row"]

    def body(*args):
        return on_device(devices, *args)

    return jax.shard_map(
        body,
        mesh=mesh,
        in_specs=(
            P("groups", "row", None),
            P(),
            P(),
            P(),
            P(),
            P(),
            P(),
            P(("groups", "row"), None, None),
            P("groups"),
            P("groups"),
        ),
        out_specs=(
            P(("groups", "row"), None, None),
            P("groups", "row", None),
            P("groups", None),
            P("groups", None),
        ),
        check_vma=False,
    )
```

```python
import jax
import jax.numpy as jnp
from jax import lax
from jax.experimental import pallas as pl
from jax.experimental.pallas import tpu as pltpu
from jax.sharding import PartitionSpec as P

PAIRED = 32
EXTRA = 8
QUAD = 4
BLOCK = 8
RANK = 32
PACKED = 80
F32 = jnp.float32
BF16 = jnp.bfloat16
SMEM = pl.BlockSpec(memory_space=pltpu.SMEM)


def vmem():
    return pl.BlockSpec(memory_space=pltpu.VMEM)


def params(mib=48):
    return pltpu.CompilerParams(vmem_limit_bytes=mib * 1024 * 1024)


def sds(shape, dtype):
    return jax.ShapeDtypeStruct(shape, dtype)


def place():
    k = lax.axis_index("row")
    return k >> 2, k & 3


def bounds_of(ref):
    ends, total = [], jnp.int32(0)
    for c in range(ref.shape[0]):
        total = total + ref[c]
        ends.append(total)
    return ends


def chain_of(residue, ends):
    chain = jnp.zeros(residue.shape, jnp.int32)
    for end in ends:
        chain = chain + jnp.where(residue >= end, 1, 0)
    return chain


def count_of(chain, hom_ref):
    picked = jnp.zeros(chain.shape, F32)
    for c in range(hom_ref.shape[0]):
        picked = jnp.where(chain == c, hom_ref[c].astype(F32), picked)
    return picked


def swap4(xs, low):
    lane = lax.broadcasted_iota(jnp.int32, xs[0].shape, 1)
    for bit, step in ((2, 2 * low), (1, low)):
        keep = (lane & step) == 0
        ys = list(xs)
        for q in range(4):
            if q & bit == 0:
                lo, hi = xs[q], xs[q | bit]
                ys[q] = jnp.where(keep, lo, pltpu.roll(hi, step, 1))
                ys[q | bit] = jnp.where(keep, pltpu.roll(lo, 128 - step, 1), hi)
        xs = ys
    return xs


def unpack(message):
    m = message.astype(F32)
    return [
        jnp.concatenate([m[0:32], m[64:72]], axis=0),
        jnp.concatenate([m[32:64], m[72:80]], axis=0),
    ]


def pack(lo, hi):
    return jnp.concatenate([lo[0:32], hi[0:32], lo[32:40], hi[32:40]], axis=0).astype(BF16)


def spread_rows(compact, chain, chains):
    rows = [compact[0:PAIRED]]
    extra = compact[PAIRED:]
    for c in range(chains):
        rows.append(jnp.where(chain == c, extra, 0.0))
    return jnp.concatenate(rows, axis=0)


def gather_rows(full, chain, chains):
    extra = jnp.zeros((EXTRA, full.shape[1]), F32)
    for c in range(chains):
        top = PAIRED + EXTRA * c
        extra = jnp.where(chain == c, full[top : top + EXTRA], extra)
    return jnp.concatenate([full[0:PAIRED], extra], axis=0)


def left_chain(a, b, ends):
    lane = lax.broadcasted_iota(jnp.int32, (EXTRA, 128), 1)
    residue = 32 * a + 8 * (b ^ (lane >> 5)) + (lane & 7)
    return jnp.concatenate([chain_of(residue, ends)] * 8, axis=1)


def right_chain(a, b, chunk, ends):
    lane = lax.broadcasted_iota(jnp.int32, (EXTRA, 256), 1)
    parts = []
    for tt in range(4):
        residue = 32 * (a ^ (4 * chunk + tt)) + 8 * b + (lane >> 5)
        parts.append(chain_of(residue, ends))
    return jnp.concatenate(parts, axis=1)


def spread_matrix():
    row = lax.broadcasted_iota(jnp.int32, (512, 512), 0)
    o = lax.broadcasted_iota(jnp.int32, (512, 512), 1)
    r, k = row >> 6, row & 63
    target = jnp.where(k < RANK, k * 8 + r, 256 + r * 32 + (k - RANK))
    return jnp.where(o == target, 1.0, 0.0).astype(BF16)


def swap_matrix():
    row = lax.broadcasted_iota(jnp.int32, (512, 512), 0)
    col = lax.broadcasted_iota(jnp.int32, (512, 512), 1)
    q, m = row >> 7, (row >> 3) & 3
    target = (m << 7) | (row & 0x67) | (q << 3)
    return jnp.where(col == target, 1.0, 0.0).astype(BF16)


def swap_blocks(o, swap):
    blocks = o.shape[1] // 128
    wide = [
        jnp.concatenate(
            [
                o[(g * 4 + q) * 32 : (g * 4 + q + 1) * 32, blk * 128 : blk * 128 + 128]
                for q in range(4)
            ],
            axis=1,
        )
        for blk in range(blocks)
        for g in range(8)
    ]
    return jnp.dot(
        jnp.concatenate(wide, axis=0), swap, preferred_element_type=F32
    ).astype(BF16)


def fetch(pairs, sems):
    copies = [pltpu.make_async_copy(a, b, sems.at[n]) for n, (a, b) in enumerate(pairs)]
    for c in copies:
        c.start()
    return copies


def start_kernel(
    x_hbm, adj_hbm, scale_hbm, shift_hbm, mat_hbm, off_hbm, len_hbm, hom_hbm, final_hbm,
    m0, m1, m2, m3, right_ref, norm_ref, hat_ref, rstd_ref, spread_ref, swap_ref, final_ref,
    x_ref, adj_ref, scale_ref, shift_ref, mat_ref, off_ref, len_ref, hom_ref,
    work, full, comp, sems,
):
    messages = (m0, m1, m2, m3)
    copies = fetch(
        [
            (adj_hbm, adj_ref), (x_hbm, x_ref), (scale_hbm, scale_ref),
            (shift_hbm, shift_ref), (mat_hbm, mat_ref), (off_hbm, off_ref),
            (len_hbm, len_ref), (hom_hbm, hom_ref), (final_hbm, final_ref),
        ],
        sems,
    )
    depth = x_ref.shape[0]
    residues = adj_ref.shape[1]
    groups = residues // 32
    a, b = place()
    spread = spread_matrix()
    spread_ref[...] = spread
    swap_ref[...] = swap_matrix()
    copies[0].wait()
    work[...] = adj_ref[...].astype(F32).reshape(BLOCK * residues, 128)
    for t in range(QUAD):

        def step(u, _, t=t):
            tiles = []
            for jj in range(BLOCK):
                j = 32 * (a ^ u) + 8 * (b ^ t) + jj
                tiles.append(work[pl.ds(j, BLOCK, stride=residues), :])
            rows = pl.ds(pl.multiple_of(u * 64, 64), 64)
            messages[t][rows, :] = jnp.concatenate(tiles, axis=0).astype(BF16)
            return 0

        lax.fori_loop(0, groups, step, 0, unroll=groups <= 4)
    for c in copies[1:8]:
        c.wait()
    x = x_ref[...].astype(F32)
    centred = x - jnp.mean(x, axis=-1, keepdims=True)
    rstd = lax.rsqrt(jnp.mean(centred * centred, axis=-1, keepdims=True) + 1e-05)
    hat = (centred * rstd).reshape(depth * BLOCK, 256)
    normed = (hat * scale_ref[...] + shift_ref[...]).astype(BF16)
    hat_ref[...] = hat
    norm_ref[...] = normed
    rstd_ref[...] = jnp.broadcast_to(rstd, (depth, BLOCK, 128)).reshape(depth * BLOCK, 128)
    proj = lax.dot_general(
        normed, mat_ref[...], (((1,), (1,)), ((), ())), preferred_element_type=F32
    ) + off_ref[...]
    full[0 : depth * BLOCK, :] = proj
    full[depth * BLOCK :, :] = jnp.zeros((EXTRA * BLOCK, 64), F32)
    comp[0 : PAIRED * BLOCK, :] = proj[0 : PAIRED * BLOCK]
    comp[PAIRED * BLOCK :, :] = chain_rows(full, a, b, len_ref, hom_ref)
    rows = PAIRED + EXTRA
    wide = jnp.concatenate([comp[pl.ds(r, rows, stride=BLOCK), :] for r in range(BLOCK)], axis=1)
    out = jnp.dot(wide.astype(BF16), spread, preferred_element_type=F32)
    left = pack(out[:, 0:128], out[:, 128:256])
    for m in messages:
        m[groups * 64 :, :] = left
    right_ref[...] = pack(out[:, 256:384], out[:, 384:512])
    copies[8].wait()


def chain_rows(full, a, b, len_ref, hom_ref):
    lanes = full.shape[1]
    residue = lax.broadcasted_iota(jnp.int32, (EXTRA * BLOCK, lanes), 0)
    entry = residue >> 3
    chain = chain_of(32 * a + 8 * b + (residue & 7), bounds_of(len_ref))
    extra = jnp.zeros((EXTRA * BLOCK, lanes), F32)
    start = jnp.int32(PAIRED)
    for c in range(len_ref.shape[0]):
        rows = full[pl.ds(pl.multiple_of(start * BLOCK, BLOCK), EXTRA * BLOCK), :]
        extra = jnp.where((chain == c) & (entry < hom_ref[c]), rows, extra)
        start = start + hom_ref[c]
    return extra


def adjoint_kernel(
    chunks, len_ref, hom_ref, final_ref, swap_ref, spread_ref, norm_ref, m0, m1, m2, m3,
    s_ref, og_ref, ft_ref, lx_ref, lt_ref, gather_ref, few_ref, nfull,
):
    messages = (m0, m1, m2, m3)
    a, b = place()
    ends = bounds_of(len_ref)
    swap = swap_ref[...]
    bottom = chunks * 256
    lx = spread_rows(
        left_lanes([m[bottom : bottom + PACKED, :] for m in messages]),
        left_chain(a, b, ends),
        len_ref.shape[0],
    )
    lx_ref[...] = lx.astype(BF16)
    lt_ref[...] = lx.T.astype(BF16)
    gather_ref[...] = spread_ref[...].astype(F32).T.astype(BF16)
    depth8 = norm_ref.shape[0]
    nfull[0:depth8, :] = norm_ref[...].astype(F32)
    nfull[depth8:, :] = jnp.zeros((EXTRA * BLOCK, 256), F32)
    few_ref[0 : PAIRED * BLOCK, :] = norm_ref[0 : PAIRED * BLOCK, :]
    few_ref[PAIRED * BLOCK :, :] = chain_rows(nfull, a, b, len_ref, hom_ref).astype(BF16)
    low = lax.broadcasted_iota(jnp.int32, (32, 128), 0)
    chain_i, inv_same = [], []
    for t in range(QUAD):
        chain = chain_of(32 * a + 8 * (b ^ t) + (low & 7), ends)
        chain_i.append(chain)
        inv_same.append(1.0 / (float(PAIRED) + count_of(chain, hom_ref) + 0.001))
    inv_other = 1.0 / jnp.full((32, 128), PAIRED + 0.001, F32)
    final = final_ref[...]
    ft_ref[...] = final.astype(F32).T.astype(BF16)

    def step(g, _):
        blocks = []
        for tt in range(4):
            u = 4 * g + tt
            for half in range(2):
                chain_j = chain_of(32 * (a ^ u) + 8 * b + 4 * half + (low >> 3), ends)
                top = pl.ds(pl.multiple_of(u * 64 + half * 32, 32), 32)
                for t in range(QUAD):
                    inv = jnp.where(chain_i[t] == chain_j, inv_same[t], inv_other)
                    blocks.append(messages[t][top, :].astype(F32) * inv)
        s = jnp.concatenate(blocks, axis=0)
        s_ref[pl.ds(pl.multiple_of(g * 1024, 1024), 1024), :] = s.astype(BF16)
        st = s.T.astype(BF16)
        for half in range(2):
            og = jnp.dot(
                final, st[:, half * 512 : half * 512 + 512], preferred_element_type=F32
            ).astype(BF16)
            moved = swap_blocks(og, swap)
            for jg in range(4):
                for jl in range(4):
                    row = ((half * 4 + jg) * 4 + jl) * 32
                    at = pl.ds(pl.multiple_of(g * 1024 + row, 32), 32)
                    for cb in range(8):
                        top = (jg * 8 + cb) * 32
                        og_ref[at, cb * 128 : cb * 128 + 128] = moved[
                            top : top + 32, jl * 128 : jl * 128 + 128
                        ]
        return 0

    lax.fori_loop(0, chunks, step, 0, unroll=chunks == 1)


def left_lanes(lefts):
    parts = [unpack(m) for m in lefts]
    lanes = []
    for h in range(2):
        lanes += swap4([parts[t][h] for t in range(QUAD)], 32)
    return jnp.concatenate(lanes, axis=1)


def right_lanes(rights):
    return jnp.concatenate([blk for m in rights for blk in unpack(m)], axis=1)


def grad_kernel(
    chunks, len_ref, og_ref, lt_ref, r3, r2, r1, r0,
    l0, l1, l2, l3, g0, g1, g2, g3, rt_ref, lg_acc,
):
    rights = (r0, r1, r2, r3)
    lefts, grads = (l0, l1, l2, l3), (g0, g1, g2, g3)
    chains = len_ref.shape[0]
    a, b = place()
    ends = bounds_of(len_ref)
    chain_l = left_chain(a, b, ends)
    lt = lt_ref[...]
    lg_acc[...] = jnp.zeros(lg_acc.shape, F32)

    def step(g, _):
        chain_r = right_chain(a, b, g, ends)
        at80 = pl.ds(pl.multiple_of(g * PACKED, 16), PACKED)
        at1024 = pl.ds(pl.multiple_of(g * 1024, 1024), 1024)
        rx = spread_rows(right_lanes([r[at80, :] for r in rights]), chain_r, chains)
        rt_ref[at1024, :] = rx.T.astype(BF16)
        og = og_ref[at1024, :]
        rg = jnp.dot(og, lt, preferred_element_type=F32).T
        rg = gather_rows(rg, chain_r, chains)
        for tt in range(4):
            grads[tt][at80, :] = pack(
                rg[:, tt * 256 : tt * 256 + 128], rg[:, tt * 256 + 128 : tt * 256 + 256]
            )
        lg_acc[...] += jnp.dot(rx.astype(BF16), og, preferred_element_type=F32)
        return 0

    lax.fori_loop(0, chunks, step, 0, unroll=chunks == 1)
    lgc = gather_rows(lg_acc[...], chain_l, chains)
    halves = []
    for h in range(2):
        xs = [lgc[:, (4 * h + q) * 128 : (4 * h + q + 1) * 128] for q in range(4)]
        halves.append(swap4(xs, 32))
    for t in range(QUAD):
        lefts[t][...] = pack(halves[0][t], halves[1][t])


def pair_kernel(
    chunks, len_ref, hom_ref, s_ref, ft_ref, swap_ref, bias_ref, lx_ref, rt_ref,
    l0, l1, l2, l3, own_ref, cross_ref, core_ref, p0, p1, px, n_buf, w_acc,
):
    lefts = (l0, l1, l2, l3)
    quads = ((own_ref, 0), (core_ref, 0), (cross_ref, 0), (core_ref, 256 + PACKED))
    pairs = ((p0, 0), (p1, 0), (px, 0), (px, chunks * 256))
    a, b = place()
    ends = bounds_of(len_ref)
    w_acc[...] = jnp.zeros(w_acc.shape, F32)
    lx = lx_ref[...]
    swap = swap_ref[...]
    bias = bias_ref[...]
    lane = lax.broadcasted_iota(jnp.int32, (8, 128), 1)
    chain_i = chain_of(32 * a + 8 * (b ^ (lane >> 5)) + (lane & 7), ends)
    same_inv = 1.0 / (float(PAIRED) + count_of(chain_i, hom_ref) + 0.001)
    other_inv = 1.0 / jnp.full((8, 128), PAIRED + 0.001, F32)

    def step(g, _):
        rt = rt_ref[pl.ds(pl.multiple_of(g * 1024, 1024), 1024), :]
        for half in range(2):
            o = jnp.dot(
                rt, lx[:, half * 512 : half * 512 + 512], preferred_element_type=F32
            ).astype(BF16)
            moved = swap_blocks(o, swap)
            for cb in range(4):
                for cl in range(4):
                    row = ((half * 4 + cb) * 4 + cl) * 32
                    for jg in range(8):
                        top = (cb * 8 + jg) * 32
                        n_buf[row : row + 32, jg * 128 : jg * 128 + 128] = moved[
                            top : top + 32, cl * 128 : cl * 128 + 128
                        ]
        n = n_buf[...]
        s = s_ref[pl.ds(pl.multiple_of(g * 1024, 1024), 1024), :]
        w_acc[...] += jnp.dot(n, s, preferred_element_type=F32)
        pt = jnp.dot(ft_ref[...], n, preferred_element_type=F32)
        tiles = []
        for tt in range(4):
            for half in range(2):
                res_j = 32 * (a ^ (4 * g + tt)) + 8 * b + 4 * half + ((lane >> 3) & 3)
                inv = jnp.where(chain_i == chain_of(res_j, ends), same_inv, other_inv)
                inv_col = jnp.broadcast_to(inv[0:1], (128, 128)).T
                blk = tt * 2 + half
                tiles.append((pt[:, blk * 128 : blk * 128 + 128].T + bias) * inv_col)
        for t in range(QUAD):
            ref, top = pairs[t]
            ref[pl.ds(pl.multiple_of(top + g * 256, 256), 256), :] = jnp.concatenate(
                [v[t * 32 : t * 32 + 32] for v in tiles], axis=0
            ).astype(BF16)
        return 0

    lax.fori_loop(0, chunks, step, 0, unroll=chunks == 1)
    for t in range(QUAD):
        ref, top = quads[t]
        ref[top + 256 : top + 256 + PACKED, :] = lefts[t][...]
        rows = pl.ds(pl.multiple_of((b ^ t) * 256, 256), 256)
        ref[top : top + 256, :] = w_acc[rows, :].astype(BF16)


def total(values):
    out = values[0].astype(F32)
    for value in values[1:]:
        out = out + value.astype(F32)
    return out


def middle_kernel(own_ref, cross_ref, core_ref, mine_ref, theirs_ref):
    rows = 256 + PACKED
    mine_ref[...] = own_ref[...].astype(F32) + core_ref[0:rows, :].astype(F32)
    theirs_ref[...] = total([cross_ref[...], core_ref[rows:, :]]).astype(BF16)


def back_kernel(groups, gather_ref, few_ref, *refs):
    quads, rgs = refs[:2], refs[2 : 2 + groups]
    pg_ref, out_ref, comp = refs[2 + groups :]
    lg = total([q[256:, :] for q in quads])
    rg = total([r[...] for r in rgs])
    wide = jnp.concatenate([blk for g in (lg, rg) for blk in unpack(g)], axis=1)
    rows = PAIRED + EXTRA
    per = jnp.dot(wide.astype(BF16), gather_ref[...], preferred_element_type=F32)
    for r in range(BLOCK):
        comp[pl.ds(r, rows, stride=BLOCK), :] = per[:, r * 64 : r * 64 + 64]
    pg = comp[...]
    pg_ref[...] = pg.astype(BF16)
    fm = jnp.dot(pg.T.astype(BF16), few_ref[...], preferred_element_type=F32)
    out_ref[...] = jnp.concatenate([fm[:, 0:128], fm[:, 128:256]], axis=0).astype(BF16)


def fold_kernel(mine_ref, theirs_ref, out_ref):
    out_ref[...] = total([mine_ref[0:256, :], theirs_ref[0:256, :]]).astype(BF16)


def join_kernel(w0, w1, fm_ref, out_ref):
    out_ref[0:256, :] = total([w0[...], w1[...]]).astype(BF16)
    out_ref[256:384, :] = fm_ref[...]


def align_kernel(
    len_ref, hom_ref, pg_ref, mat_ref, scale_ref, hat_ref, rstd_ref, out_ref, full
):
    a, b = place()
    depth8 = hat_ref.shape[0]
    full[0 : PAIRED * BLOCK, :] = pg_ref[0 : PAIRED * BLOCK, :].astype(F32)
    full[PAIRED * BLOCK :, :] = jnp.zeros((full.shape[0] - PAIRED * BLOCK, 64), F32)
    extra = pg_ref[PAIRED * BLOCK :, :].astype(F32)
    residue = lax.broadcasted_iota(jnp.int32, (EXTRA * BLOCK, 64), 0)
    entry = residue >> 3
    chain = chain_of(32 * a + 8 * b + (residue & 7), bounds_of(len_ref))
    start = jnp.int32(PAIRED)
    for c in range(len_ref.shape[0]):
        at = pl.ds(pl.multiple_of(start * BLOCK, BLOCK), EXTRA * BLOCK)
        full[at, :] += jnp.where((chain == c) & (entry < hom_ref[c]), extra, 0.0)
        start = start + hom_ref[c]
    g = jnp.dot(full[0:depth8, :].astype(BF16), mat_ref[...], preferred_element_type=F32)
    g = g * scale_ref[...]
    hat = hat_ref[...]
    m1 = jnp.mean(g, axis=-1, keepdims=True)
    m2 = jnp.mean(g * hat, axis=-1, keepdims=True)
    rstd = rstd_ref[...]
    dx = (g - m1 - hat * m2) * jnp.concatenate([rstd, rstd], axis=1)
    out_ref[...] = dx.reshape(out_ref.shape).astype(BF16)


def assemble_kernel(*refs):
    pieces, out_ref, work = refs[:QUAD], refs[QUAD], refs[QUAD + 1]
    residues = out_ref.shape[1]
    groups = residues // 32
    tops = (0, 0, 0, groups * 64)
    a, b = place()
    for t in range(QUAD):

        def step(u, _, t=t):
            tile = pieces[t][pl.ds(pl.multiple_of(tops[t] + u * 64, 64), 64), :].astype(F32)
            for jj in range(BLOCK):
                j = 32 * (a ^ u) + 8 * (b ^ t) + jj
                work[pl.ds(j, BLOCK, stride=residues), :] = tile[jj * 8 : jj * 8 + 8]
            return 0

        lax.fori_loop(0, groups, step, 0, unroll=groups <= 4)
    out_ref[...] = work[...].reshape(out_ref.shape).astype(BF16)


def merge_kernel(*refs):
    out_ref, fms = refs[-1], refs[:-1]
    out_ref[0:256, :] = total([fms[0][0:256, :], fms[1][0:256, :]]).astype(BF16)
    out_ref[256:384, :] = total([f[f.shape[0] - 128 :, :] for f in fms]).astype(BF16)


def final_kernel(m0, m1, m2, m3, w_ref, fm_ref):
    _, b = place()
    for t, m in enumerate((m0, m1, m2, m3)):
        rows = pl.ds(pl.multiple_of((b ^ t) * 256, 256), 256)
        w_ref[rows, :] = m[0:256, :].astype(F32)
    fm = total([m[256:384, :] for m in (m0, m1, m2, m3)])
    fm_ref[...] = jnp.concatenate([fm[0:64], fm[64:128]], axis=1)


HBM = pl.BlockSpec(memory_space=pltpu.HBM)


def call(kernel, outs, ins, in_specs=None, out_specs=None, scratch=(), work=0, mib=48):
    many = isinstance(outs, (list, tuple))
    if in_specs is not None:
        ins = [
            pltpu.with_memory_space_constraint(v, pltpu.HBM) if spec is HBM else v
            for v, spec in zip(ins, in_specs)
        ]
    return pl.pallas_call(
        kernel,
        out_shape=outs,
        in_specs=in_specs if in_specs is not None else [vmem()] * len(ins),
        out_specs=out_specs or ([vmem()] * len(outs) if many else vmem()),
        scratch_shapes=list(scratch),
        compiler_params=params(mib),
        cost_estimate=pl.CostEstimate(flops=work, bytes_accessed=work // 500, transcendentals=0),
    )(*ins)


def on_device(
    devices, x, scale, shift, mat, off, final, bias, adjoint, lengths, homologs
):
    groups = devices // QUAD
    chunks = groups // 4
    residues = adjoint.shape[1]
    depth = x.shape[0]
    scale, shift, off, bias = scale[None], shift[None], off[None], bias[None]
    mat = mat.T

    def near(value, t):
        return lax.ppermute(value, "row", [(k, k ^ t) for k in range(devices)])

    def far(value, u):
        return lax.ppermute(value, "row", [(k, k ^ (4 * u)) for k in range(devices)])

    def quad(parts):
        return [parts[0]] + [near(parts[t], t) for t in range(1, QUAD)]

    def by_slot(parts):
        if chunks == 1:
            return parts
        return [jnp.concatenate(parts[s::4], axis=0) for s in range(4)]

    def from_slot(parts, rows):
        if chunks == 1:
            return parts
        return [parts[u % 4][(u // 4) * rows : (u // 4 + 1) * rows] for u in range(groups)]

    *messages, right, normed, hat, rstd, spread, swap, final = call(
        start_kernel,
        [sds((groups * 64 + PACKED, 128), BF16)] * QUAD
        + [
            sds((PACKED, 128), BF16),
            sds((depth * BLOCK, 256), BF16),
            sds((depth * BLOCK, 256), F32),
            sds((depth * BLOCK, 128), F32),
            sds((512, 512), BF16),
            sds((512, 512), BF16),
            sds(final.shape, BF16),
        ],
        [x, adjoint, scale, shift, mat, off, lengths, homologs, final],
        in_specs=[HBM] * 9,
        scratch=[
            pltpu.VMEM(x.shape, BF16),
            pltpu.VMEM(adjoint.shape, BF16),
            pltpu.VMEM((1, 256), F32),
            pltpu.VMEM((1, 256), F32),
            pltpu.VMEM((64, 256), BF16),
            pltpu.VMEM((1, 64), F32),
            pltpu.SMEM(lengths.shape, jnp.int32),
            pltpu.SMEM(homologs.shape, jnp.int32),
            pltpu.VMEM((BLOCK * residues, 128), F32),
            pltpu.VMEM(((depth + EXTRA) * BLOCK, 64), F32),
            pltpu.VMEM(((PAIRED + EXTRA) * BLOCK, 64), F32),
            pltpu.SemaphoreType.DMA((9,)),
        ],
        work=10**9,
    )
    messages = quad(messages)
    rights = by_slot([right] + [far(right, u) for u in range(1, groups)])

    s, og, final_t, lx, lt, gather, few = call(
        lambda *refs: adjoint_kernel(chunks, *refs),
        [
            sds((chunks * 1024, 128), BF16),
            sds((chunks * 1024, 1024), BF16),
            sds((128, 1024), BF16),
            sds((128, 1024), BF16),
            sds((1024, 128), BF16),
            sds((512, 512), BF16),
            sds(((PAIRED + EXTRA) * BLOCK, 256), BF16),
        ],
        [lengths, homologs, final, swap, spread, normed, *messages],
        in_specs=[SMEM] * 2 + [vmem()] * (4 + QUAD),
        scratch=[pltpu.VMEM(((depth + EXTRA) * BLOCK, 256), F32)],
        work=2 * 10**9,
    )

    outs = call(
        lambda *refs: grad_kernel(chunks, *refs),
        [sds((PACKED, 128), BF16)] * QUAD
        + [sds((chunks * PACKED, 128), BF16)] * 4
        + [sds((chunks * 1024, 128), BF16)],
        [lengths, og, lt, *rights[::-1]],
        in_specs=[SMEM] + [vmem()] * (2 + QUAD),
        scratch=[pltpu.VMEM((128, 1024), F32)],
        work=2 * 10**9,
    )
    lgs, rgs, rt = outs[0:4], list(outs[4:8]), outs[8]
    rgs = from_slot(rgs, PACKED)
    rgs = [rgs[0]] + [far(rgs[u], u) for u in range(1, groups)]
    own, cross, core, pair_own, pair_core, pair_cross = call(
        lambda *refs: pair_kernel(chunks, *refs),
        [sds((256 + PACKED, 128), BF16)] * 2
        + [sds((512 + 2 * PACKED, 128), BF16)]
        + [sds((groups * 64, 128), BF16)] * 2
        + [sds((groups * 128, 128), BF16)],
        [lengths, homologs, s, final_t, swap, bias, lx, rt, *lgs],
        in_specs=[SMEM] * 2 + [vmem()] * (6 + QUAD),
        scratch=[pltpu.VMEM((1024, 1024), BF16), pltpu.VMEM((1024, 128), F32)],
        work=4 * 10**9,
    )
    core = near(core, 1)
    mine, theirs = call(
        middle_kernel,
        [sds((256 + PACKED, 128), F32), sds((256 + PACKED, 128), BF16)],
        [own, cross, core],
        work=10**7,
    )
    quads = [mine, near(theirs, 2)]

    pg, fm = call(
        lambda *refs: back_kernel(groups, *refs),
        [sds(((PAIRED + EXTRA) * BLOCK, 64), BF16), sds((128, 128), BF16)],
        [gather, few, *quads, *rgs],
        scratch=[pltpu.VMEM(((PAIRED + EXTRA) * BLOCK, 64), F32)],
        work=10**9,
    )
    half = groups // 2
    w = call(fold_kernel, sds((256, 128), BF16), quads, work=10**7)
    steps = [half >> k for k in range(half.bit_length() - 1)]
    for u in steps[:-1]:
        w = call(fold_kernel, sds((256, 128), BF16), [w, far(w, u)], work=10**7)
    part = call(join_kernel, sds((384, 128), BF16), [w, far(w, steps[-1]), fm], work=10**7)
    parts = [part] + [far(part if u == 1 else fm, u) for u in range(1, groups)]
    pair_cross = near(pair_cross, 2)
    pairs = [pair_own, near(pair_core, 1), pair_cross, near(pair_cross, 1)]
    alignment_gradient = call(
        align_kernel,
        sds(x.shape, BF16),
        [lengths, homologs, pg, mat, scale, hat, rstd],
        in_specs=[SMEM] * 2 + [vmem()] * 5,
        scratch=[pltpu.VMEM(((depth + EXTRA) * BLOCK, 64), F32)],
        work=10**9,
    )
    pair_delta = call(
        assemble_kernel,
        sds(adjoint.shape, BF16),
        pairs,
        scratch=[pltpu.VMEM((BLOCK * residues, 128), F32)],
        work=10**9,
    )
    parts, alignment_gradient, pair_delta = lax.optimization_barrier(
        (parts, alignment_gradient, pair_delta)
    )
    merged = call(
        merge_kernel, sds((384, 128), BF16), parts, work=10**7
    )
    cross = near(merged, 2)
    w, fm = call(
        final_kernel,
        [sds((1024, 128), F32), sds((64, 256), F32)],
        [merged, near(merged, 1), cross, near(cross, 1)],
        work=10**8,
    )
    return pair_delta, alignment_gradient, w, fm.T


def solution(mesh):
    devices = mesh.shape["row"]

    def body(*args):
        return on_device(devices, *args)

    return jax.shard_map(
        body,
        mesh=mesh,
        in_specs=(
            P("groups", "row", None),
            P(),
            P(),
            P(),
            P(),
            P(),
            P(),
            P(("groups", "row"), None, None),
            P("groups"),
            P("groups"),
        ),
        out_specs=(
            P(("groups", "row"), None, None),
            P("groups", "row", None),
            P("groups", None),
            P("groups", None),
        ),
        check_vma=False,
    )
```

```python
import jax
import jax.numpy as jnp
from jax import lax
from jax.experimental import pallas as pl
from jax.experimental.pallas import tpu as pltpu
from jax.sharding import PartitionSpec as P

PAIRED = 32
EXTRA = 8
QUAD = 4
BLOCK = 8
RANK = 32
PACKED = 80
F32 = jnp.float32
BF16 = jnp.bfloat16
SMEM = pl.BlockSpec(memory_space=pltpu.SMEM)


def vmem():
    return pl.BlockSpec(memory_space=pltpu.VMEM)


def params(mib=48):
    return pltpu.CompilerParams(vmem_limit_bytes=mib * 1024 * 1024)


def sds(shape, dtype):
    return jax.ShapeDtypeStruct(shape, dtype)


def place():
    k = lax.axis_index("row")
    return k >> 2, k & 3


def bounds_of(ref):
    ends, total = [], jnp.int32(0)
    for c in range(ref.shape[0]):
        total = total + ref[c]
        ends.append(total)
    return ends


def chain_of(residue, ends):
    chain = jnp.zeros(residue.shape, jnp.int32)
    for end in ends:
        chain = chain + jnp.where(residue >= end, 1, 0)
    return chain


def count_of(chain, hom_ref):
    picked = jnp.zeros(chain.shape, F32)
    for c in range(hom_ref.shape[0]):
        picked = jnp.where(chain == c, hom_ref[c].astype(F32), picked)
    return picked


def swap4(xs, low):
    lane = lax.broadcasted_iota(jnp.int32, xs[0].shape, 1)
    for bit, step in ((2, 2 * low), (1, low)):
        keep = (lane & step) == 0
        ys = list(xs)
        for q in range(4):
            if q & bit == 0:
                lo, hi = xs[q], xs[q | bit]
                ys[q] = jnp.where(keep, lo, pltpu.roll(hi, step, 1))
                ys[q | bit] = jnp.where(keep, pltpu.roll(lo, 128 - step, 1), hi)
        xs = ys
    return xs


def unpack(message):
    m = message.astype(F32)
    return [
        jnp.concatenate([m[0:32], m[64:72]], axis=0),
        jnp.concatenate([m[32:64], m[72:80]], axis=0),
    ]


def pack(lo, hi):
    return jnp.concatenate([lo[0:32], hi[0:32], lo[32:40], hi[32:40]], axis=0).astype(BF16)


def spread_rows(compact, chain, chains):
    rows = [compact[0:PAIRED]]
    extra = compact[PAIRED:]
    for c in range(chains):
        rows.append(jnp.where(chain == c, extra, 0.0))
    return jnp.concatenate(rows, axis=0)


def gather_rows(full, chain, chains):
    extra = jnp.zeros((EXTRA, full.shape[1]), F32)
    for c in range(chains):
        top = PAIRED + EXTRA * c
        extra = jnp.where(chain == c, full[top : top + EXTRA], extra)
    return jnp.concatenate([full[0:PAIRED], extra], axis=0)


def left_chain(a, b, ends):
    lane = lax.broadcasted_iota(jnp.int32, (EXTRA, 128), 1)
    residue = 32 * a + 8 * (b ^ (lane >> 5)) + (lane & 7)
    return jnp.concatenate([chain_of(residue, ends)] * 8, axis=1)


def right_chain(a, b, chunk, ends):
    lane = lax.broadcasted_iota(jnp.int32, (EXTRA, 256), 1)
    parts = []
    for tt in range(4):
        residue = 32 * (a ^ (4 * chunk + tt)) + 8 * b + (lane >> 5)
        parts.append(chain_of(residue, ends))
    return jnp.concatenate(parts, axis=1)


def spread_matrix():
    row = lax.broadcasted_iota(jnp.int32, (512, 512), 0)
    o = lax.broadcasted_iota(jnp.int32, (512, 512), 1)
    r, k = row >> 6, row & 63
    target = jnp.where(k < RANK, k * 8 + r, 256 + r * 32 + (k - RANK))
    return jnp.where(o == target, 1.0, 0.0).astype(BF16)


def swap_matrix():
    row = lax.broadcasted_iota(jnp.int32, (512, 512), 0)
    col = lax.broadcasted_iota(jnp.int32, (512, 512), 1)
    q, m = row >> 7, (row >> 3) & 3
    target = (m << 7) | (row & 0x67) | (q << 3)
    return jnp.where(col == target, 1.0, 0.0).astype(BF16)


def swap_blocks(o, swap):
    blocks = o.shape[1] // 128
    wide = [
        jnp.concatenate(
            [
                o[(g * 4 + q) * 32 : (g * 4 + q + 1) * 32, blk * 128 : blk * 128 + 128]
                for q in range(4)
            ],
            axis=1,
        )
        for blk in range(blocks)
        for g in range(8)
    ]
    return jnp.dot(
        jnp.concatenate(wide, axis=0), swap, preferred_element_type=F32
    ).astype(BF16)


def fetch(pairs, sems):
    copies = [pltpu.make_async_copy(a, b, sems.at[n]) for n, (a, b) in enumerate(pairs)]
    for c in copies:
        c.start()
    return copies


def start_kernel(
    x_hbm, adj_hbm, scale_hbm, shift_hbm, mat_hbm, off_hbm, len_hbm, hom_hbm, final_hbm,
    m0, m1, m2, m3, right_ref, norm_ref, x_ref, spread_ref, swap_ref, final_ref,
    adj_ref, scale_ref, shift_ref, mat_ref, off_ref, len_ref, hom_ref,
    work, full, comp, sems,
):
    messages = (m0, m1, m2, m3)
    copies = fetch(
        [
            (adj_hbm, adj_ref), (x_hbm, x_ref), (scale_hbm, scale_ref),
            (shift_hbm, shift_ref), (mat_hbm, mat_ref), (off_hbm, off_ref),
            (len_hbm, len_ref), (hom_hbm, hom_ref), (final_hbm, final_ref),
        ],
        sems,
    )
    depth = x_ref.shape[0]
    residues = adj_ref.shape[1]
    groups = residues // 32
    a, b = place()
    spread = spread_matrix()
    spread_ref[...] = spread
    swap_ref[...] = swap_matrix()
    copies[0].wait()
    work[...] = adj_ref[...].astype(F32).reshape(BLOCK * residues, 128)
    for t in range(QUAD):

        def step(u, _, t=t):
            tiles = []
            for jj in range(BLOCK):
                j = 32 * (a ^ u) + 8 * (b ^ t) + jj
                tiles.append(work[pl.ds(j, BLOCK, stride=residues), :])
            rows = pl.ds(pl.multiple_of(u * 64, 64), 64)
            messages[t][rows, :] = jnp.concatenate(tiles, axis=0).astype(BF16)
            return 0

        lax.fori_loop(0, groups, step, 0, unroll=groups <= 4)
    for c in copies[1:8]:
        c.wait()
    x = x_ref[...].astype(F32)
    centred = x - jnp.mean(x, axis=-1, keepdims=True)
    rstd = lax.rsqrt(jnp.mean(centred * centred, axis=-1, keepdims=True) + 1e-05)
    hat = (centred * rstd).reshape(depth * BLOCK, 256)
    normed = (hat * scale_ref[...] + shift_ref[...]).astype(BF16)
    norm_ref[...] = normed
    proj = lax.dot_general(
        normed, mat_ref[...], (((1,), (1,)), ((), ())), preferred_element_type=F32
    ) + off_ref[...]
    full[0 : depth * BLOCK, :] = proj
    full[depth * BLOCK :, :] = jnp.zeros((EXTRA * BLOCK, 64), F32)
    comp[0 : PAIRED * BLOCK, :] = proj[0 : PAIRED * BLOCK]
    comp[PAIRED * BLOCK :, :] = chain_rows(full, a, b, len_ref, hom_ref)
    rows = PAIRED + EXTRA
    wide = jnp.concatenate([comp[pl.ds(r, rows, stride=BLOCK), :] for r in range(BLOCK)], axis=1)
    out = jnp.dot(wide.astype(BF16), spread, preferred_element_type=F32)
    left = pack(out[:, 0:128], out[:, 128:256])
    for m in messages:
        m[groups * 64 :, :] = left
    right_ref[...] = pack(out[:, 256:384], out[:, 384:512])
    copies[8].wait()


def chain_rows(full, a, b, len_ref, hom_ref):
    lanes = full.shape[1]
    residue = lax.broadcasted_iota(jnp.int32, (EXTRA * BLOCK, lanes), 0)
    entry = residue >> 3
    chain = chain_of(32 * a + 8 * b + (residue & 7), bounds_of(len_ref))
    extra = jnp.zeros((EXTRA * BLOCK, lanes), F32)
    start = jnp.int32(PAIRED)
    for c in range(len_ref.shape[0]):
        rows = full[pl.ds(pl.multiple_of(start * BLOCK, BLOCK), EXTRA * BLOCK), :]
        extra = jnp.where((chain == c) & (entry < hom_ref[c]), rows, extra)
        start = start + hom_ref[c]
    return extra


def adjoint_kernel(
    chunks, len_ref, hom_ref, final_ref, swap_ref, spread_ref, norm_ref, m0, m1, m2, m3,
    s_ref, og_ref, ft_ref, lx_ref, lt_ref, gather_ref, few_ref, nfull,
):
    messages = (m0, m1, m2, m3)
    a, b = place()
    ends = bounds_of(len_ref)
    swap = swap_ref[...]
    bottom = chunks * 256
    lx = spread_rows(
        left_lanes([m[bottom : bottom + PACKED, :] for m in messages]),
        left_chain(a, b, ends),
        len_ref.shape[0],
    )
    lx_ref[...] = lx.astype(BF16)
    lt_ref[...] = lx.T.astype(BF16)
    gather_ref[...] = spread_ref[...].astype(F32).T.astype(BF16)
    depth8 = norm_ref.shape[0]
    nfull[0:depth8, :] = norm_ref[...].astype(F32)
    nfull[depth8:, :] = jnp.zeros((EXTRA * BLOCK, 256), F32)
    few_ref[0 : PAIRED * BLOCK, :] = norm_ref[0 : PAIRED * BLOCK, :]
    few_ref[PAIRED * BLOCK :, :] = chain_rows(nfull, a, b, len_ref, hom_ref).astype(BF16)
    low = lax.broadcasted_iota(jnp.int32, (32, 128), 0)
    chain_i, inv_same = [], []
    for t in range(QUAD):
        chain = chain_of(32 * a + 8 * (b ^ t) + (low & 7), ends)
        chain_i.append(chain)
        inv_same.append(1.0 / (float(PAIRED) + count_of(chain, hom_ref) + 0.001))
    inv_other = 1.0 / jnp.full((32, 128), PAIRED + 0.001, F32)
    final = final_ref[...]
    ft_ref[...] = final.astype(F32).T.astype(BF16)

    def step(g, _):
        blocks = []
        for tt in range(4):
            u = 4 * g + tt
            for half in range(2):
                chain_j = chain_of(32 * (a ^ u) + 8 * b + 4 * half + (low >> 3), ends)
                top = pl.ds(pl.multiple_of(u * 64 + half * 32, 32), 32)
                for t in range(QUAD):
                    inv = jnp.where(chain_i[t] == chain_j, inv_same[t], inv_other)
                    blocks.append(messages[t][top, :].astype(F32) * inv)
        s = jnp.concatenate(blocks, axis=0)
        s_ref[pl.ds(pl.multiple_of(g * 1024, 1024), 1024), :] = s.astype(BF16)
        st = s.T.astype(BF16)
        for half in range(2):
            og = jnp.dot(
                final, st[:, half * 512 : half * 512 + 512], preferred_element_type=F32
            ).astype(BF16)
            moved = swap_blocks(og, swap)
            for jg in range(4):
                for jl in range(4):
                    row = ((half * 4 + jg) * 4 + jl) * 32
                    at = pl.ds(pl.multiple_of(g * 1024 + row, 32), 32)
                    for cb in range(8):
                        top = (jg * 8 + cb) * 32
                        og_ref[at, cb * 128 : cb * 128 + 128] = moved[
                            top : top + 32, jl * 128 : jl * 128 + 128
                        ]
        return 0

    lax.fori_loop(0, chunks, step, 0, unroll=chunks == 1)


def left_lanes(lefts):
    parts = [unpack(m) for m in lefts]
    lanes = []
    for h in range(2):
        lanes += swap4([parts[t][h] for t in range(QUAD)], 32)
    return jnp.concatenate(lanes, axis=1)


def right_lanes(rights):
    return jnp.concatenate([blk for m in rights for blk in unpack(m)], axis=1)


def grad_kernel(
    chunks, len_ref, og_ref, lt_ref, r3, r2, r1, r0,
    l0, l1, l2, l3, g0, g1, g2, g3, rt_ref, lg_acc,
):
    rights = (r0, r1, r2, r3)
    lefts, grads = (l0, l1, l2, l3), (g0, g1, g2, g3)
    chains = len_ref.shape[0]
    a, b = place()
    ends = bounds_of(len_ref)
    chain_l = left_chain(a, b, ends)
    lt = lt_ref[...]
    lg_acc[...] = jnp.zeros(lg_acc.shape, F32)

    def step(g, _):
        chain_r = right_chain(a, b, g, ends)
        at80 = pl.ds(pl.multiple_of(g * PACKED, 16), PACKED)
        at1024 = pl.ds(pl.multiple_of(g * 1024, 1024), 1024)
        rx = spread_rows(right_lanes([r[at80, :] for r in rights]), chain_r, chains)
        rt_ref[at1024, :] = rx.T.astype(BF16)
        og = og_ref[at1024, :]
        rg = jnp.dot(og, lt, preferred_element_type=F32).T
        rg = gather_rows(rg, chain_r, chains)
        for tt in range(4):
            grads[tt][at80, :] = pack(
                rg[:, tt * 256 : tt * 256 + 128], rg[:, tt * 256 + 128 : tt * 256 + 256]
            )
        lg_acc[...] += jnp.dot(rx.astype(BF16), og, preferred_element_type=F32)
        return 0

    lax.fori_loop(0, chunks, step, 0, unroll=chunks == 1)
    lgc = gather_rows(lg_acc[...], chain_l, chains)
    halves = []
    for h in range(2):
        xs = [lgc[:, (4 * h + q) * 128 : (4 * h + q + 1) * 128] for q in range(4)]
        halves.append(swap4(xs, 32))
    for t in range(QUAD):
        lefts[t][...] = pack(halves[0][t], halves[1][t])


def pair_kernel(
    chunks, len_ref, hom_ref, s_ref, ft_ref, swap_ref, bias_ref, lx_ref, rt_ref,
    l0, l1, l2, l3, own_ref, cross_ref, core_ref, p0, p1, px, n_buf, w_acc,
):
    lefts = (l0, l1, l2, l3)
    quads = ((own_ref, 0), (core_ref, 0), (cross_ref, 0), (core_ref, 256 + PACKED))
    pairs = ((p0, 0), (p1, 0), (px, 0), (px, chunks * 256))
    a, b = place()
    ends = bounds_of(len_ref)
    w_acc[...] = jnp.zeros(w_acc.shape, F32)
    lx = lx_ref[...]
    swap = swap_ref[...]
    bias = bias_ref[...]
    lane = lax.broadcasted_iota(jnp.int32, (8, 128), 1)
    chain_i = chain_of(32 * a + 8 * (b ^ (lane >> 5)) + (lane & 7), ends)
    same_inv = 1.0 / (float(PAIRED) + count_of(chain_i, hom_ref) + 0.001)
    other_inv = 1.0 / jnp.full((8, 128), PAIRED + 0.001, F32)

    def step(g, _):
        rt = rt_ref[pl.ds(pl.multiple_of(g * 1024, 1024), 1024), :]
        for half in range(2):
            o = jnp.dot(
                rt, lx[:, half * 512 : half * 512 + 512], preferred_element_type=F32
            ).astype(BF16)
            moved = swap_blocks(o, swap)
            for cb in range(4):
                for cl in range(4):
                    row = ((half * 4 + cb) * 4 + cl) * 32
                    for jg in range(8):
                        top = (cb * 8 + jg) * 32
                        n_buf[row : row + 32, jg * 128 : jg * 128 + 128] = moved[
                            top : top + 32, cl * 128 : cl * 128 + 128
                        ]
        n = n_buf[...]
        s = s_ref[pl.ds(pl.multiple_of(g * 1024, 1024), 1024), :]
        w_acc[...] += jnp.dot(n, s, preferred_element_type=F32)
        pt = jnp.dot(ft_ref[...], n, preferred_element_type=F32)
        tiles = []
        for tt in range(4):
            for half in range(2):
                res_j = 32 * (a ^ (4 * g + tt)) + 8 * b + 4 * half + ((lane >> 3) & 3)
                inv = jnp.where(chain_i == chain_of(res_j, ends), same_inv, other_inv)
                inv_col = jnp.broadcast_to(inv[0:1], (128, 128)).T
                blk = tt * 2 + half
                tiles.append((pt[:, blk * 128 : blk * 128 + 128].T + bias) * inv_col)
        for t in range(QUAD):
            ref, top = pairs[t]
            ref[pl.ds(pl.multiple_of(top + g * 256, 256), 256), :] = jnp.concatenate(
                [v[t * 32 : t * 32 + 32] for v in tiles], axis=0
            ).astype(BF16)
        return 0

    lax.fori_loop(0, chunks, step, 0, unroll=chunks == 1)
    for t in range(QUAD):
        ref, top = quads[t]
        ref[top + 256 : top + 256 + PACKED, :] = lefts[t][...]
        rows = pl.ds(pl.multiple_of((b ^ t) * 256, 256), 256)
        ref[top : top + 256, :] = w_acc[rows, :].astype(BF16)


def total(values):
    out = values[0].astype(F32)
    for value in values[1:]:
        out = out + value.astype(F32)
    return out


def middle_kernel(own_ref, cross_ref, core_ref, mine_ref, theirs_ref):
    rows = 256 + PACKED
    mine_ref[...] = own_ref[...].astype(F32) + core_ref[0:rows, :].astype(F32)
    theirs_ref[...] = total([cross_ref[...], core_ref[rows:, :]]).astype(BF16)


def back_kernel(groups, gather_ref, few_ref, *refs):
    quads, rgs = refs[:2], refs[2 : 2 + groups]
    pg_ref, out_ref, comp = refs[2 + groups :]
    lg = total([q[256:, :] for q in quads])
    rg = total([r[...] for r in rgs])
    wide = jnp.concatenate([blk for g in (lg, rg) for blk in unpack(g)], axis=1)
    rows = PAIRED + EXTRA
    per = jnp.dot(wide.astype(BF16), gather_ref[...], preferred_element_type=F32)
    for r in range(BLOCK):
        comp[pl.ds(r, rows, stride=BLOCK), :] = per[:, r * 64 : r * 64 + 64]
    pg = comp[...]
    pg_ref[...] = pg.astype(BF16)
    fm = jnp.dot(pg.T.astype(BF16), few_ref[...], preferred_element_type=F32)
    out_ref[...] = jnp.concatenate([fm[:, 0:128], fm[:, 128:256]], axis=0).astype(BF16)


def fold_kernel(mine_ref, theirs_ref, out_ref):
    out_ref[...] = total([mine_ref[0:256, :], theirs_ref[0:256, :]]).astype(BF16)


def join_kernel(w0, w1, fm_ref, out_ref):
    out_ref[0:256, :] = total([w0[...], w1[...]]).astype(BF16)
    out_ref[256:384, :] = fm_ref[...]


def align_kernel(
    len_ref, hom_ref, pg_ref, mat_ref, scale_ref, x_ref, out_ref, full
):
    a, b = place()
    depth8 = x_ref.shape[0] * BLOCK
    full[0 : PAIRED * BLOCK, :] = pg_ref[0 : PAIRED * BLOCK, :].astype(F32)
    full[PAIRED * BLOCK :, :] = jnp.zeros((full.shape[0] - PAIRED * BLOCK, 64), F32)
    extra = pg_ref[PAIRED * BLOCK :, :].astype(F32)
    residue = lax.broadcasted_iota(jnp.int32, (EXTRA * BLOCK, 64), 0)
    entry = residue >> 3
    chain = chain_of(32 * a + 8 * b + (residue & 7), bounds_of(len_ref))
    start = jnp.int32(PAIRED)
    for c in range(len_ref.shape[0]):
        at = pl.ds(pl.multiple_of(start * BLOCK, BLOCK), EXTRA * BLOCK)
        full[at, :] += jnp.where((chain == c) & (entry < hom_ref[c]), extra, 0.0)
        start = start + hom_ref[c]
    g = jnp.dot(full[0:depth8, :].astype(BF16), mat_ref[...], preferred_element_type=F32)
    g = g * scale_ref[...]
    x = x_ref[...].astype(F32).reshape(depth8, 256)
    centred = x - jnp.mean(x, axis=-1, keepdims=True)
    rstd = lax.rsqrt(jnp.mean(centred * centred, axis=-1, keepdims=True) + 1e-05)
    hat = centred * rstd
    m1 = jnp.mean(g, axis=-1, keepdims=True)
    m2 = jnp.mean(g * hat, axis=-1, keepdims=True)
    dx = (g - m1 - hat * m2) * rstd
    out_ref[...] = dx.reshape(out_ref.shape).astype(BF16)


def assemble_kernel(*refs):
    pieces, out_ref, work = refs[:QUAD], refs[QUAD], refs[QUAD + 1]
    residues = out_ref.shape[1]
    groups = residues // 32
    tops = (0, 0, 0, groups * 64)
    a, b = place()
    for t in range(QUAD):

        def step(u, _, t=t):
            tile = pieces[t][pl.ds(pl.multiple_of(tops[t] + u * 64, 64), 64), :].astype(F32)
            for jj in range(BLOCK):
                j = 32 * (a ^ u) + 8 * (b ^ t) + jj
                work[pl.ds(j, BLOCK, stride=residues), :] = tile[jj * 8 : jj * 8 + 8]
            return 0

        lax.fori_loop(0, groups, step, 0, unroll=groups <= 4)
    out_ref[...] = work[...].reshape(out_ref.shape).astype(BF16)


def merge_kernel(*refs):
    out_ref, fms = refs[-1], refs[:-1]
    out_ref[0:256, :] = total([fms[0][0:256, :], fms[1][0:256, :]]).astype(BF16)
    out_ref[256:384, :] = total([f[f.shape[0] - 128 :, :] for f in fms]).astype(BF16)


def final_kernel(m0, m1, m2, m3, w_ref, fm_ref):
    _, b = place()
    for t, m in enumerate((m0, m1, m2, m3)):
        rows = pl.ds(pl.multiple_of((b ^ t) * 256, 256), 256)
        w_ref[rows, :] = m[0:256, :].astype(F32)
    fm = total([m[256:384, :] for m in (m0, m1, m2, m3)])
    fm_ref[...] = jnp.concatenate([fm[0:64], fm[64:128]], axis=1)


HBM = pl.BlockSpec(memory_space=pltpu.HBM)


def call(kernel, outs, ins, in_specs=None, out_specs=None, scratch=(), work=0, mib=48):
    many = isinstance(outs, (list, tuple))
    if in_specs is not None:
        ins = [
            pltpu.with_memory_space_constraint(v, pltpu.HBM) if spec is HBM else v
            for v, spec in zip(ins, in_specs)
        ]
    return pl.pallas_call(
        kernel,
        out_shape=outs,
        in_specs=in_specs if in_specs is not None else [vmem()] * len(ins),
        out_specs=out_specs or ([vmem()] * len(outs) if many else vmem()),
        scratch_shapes=list(scratch),
        compiler_params=params(mib),
        cost_estimate=pl.CostEstimate(flops=work, bytes_accessed=work // 500, transcendentals=0),
    )(*ins)


def on_device(
    devices, x, scale, shift, mat, off, final, bias, adjoint, lengths, homologs
):
    groups = devices // QUAD
    chunks = groups // 4
    residues = adjoint.shape[1]
    depth = x.shape[0]
    scale, shift, off, bias = scale[None], shift[None], off[None], bias[None]
    mat = mat.T

    def near(value, t):
        return lax.ppermute(value, "row", [(k, k ^ t) for k in range(devices)])

    def far(value, u):
        return lax.ppermute(value, "row", [(k, k ^ (4 * u)) for k in range(devices)])

    def quad(parts):
        return [parts[0]] + [near(parts[t], t) for t in range(1, QUAD)]

    def by_slot(parts):
        if chunks == 1:
            return parts
        return [jnp.concatenate(parts[s::4], axis=0) for s in range(4)]

    def from_slot(parts, rows):
        if chunks == 1:
            return parts
        return [parts[u % 4][(u // 4) * rows : (u // 4 + 1) * rows] for u in range(groups)]

    *messages, right, normed, x, spread, swap, final = call(
        start_kernel,
        [sds((groups * 64 + PACKED, 128), BF16)] * QUAD
        + [
            sds((PACKED, 128), BF16),
            sds((depth * BLOCK, 256), BF16),
            sds(x.shape, BF16),
            sds((512, 512), BF16),
            sds((512, 512), BF16),
            sds(final.shape, BF16),
        ],
        [x, adjoint, scale, shift, mat, off, lengths, homologs, final],
        in_specs=[HBM] * 9,
        scratch=[
            pltpu.VMEM(adjoint.shape, BF16),
            pltpu.VMEM((1, 256), F32),
            pltpu.VMEM((1, 256), F32),
            pltpu.VMEM((64, 256), BF16),
            pltpu.VMEM((1, 64), F32),
            pltpu.SMEM(lengths.shape, jnp.int32),
            pltpu.SMEM(homologs.shape, jnp.int32),
            pltpu.VMEM((BLOCK * residues, 128), F32),
            pltpu.VMEM(((depth + EXTRA) * BLOCK, 64), F32),
            pltpu.VMEM(((PAIRED + EXTRA) * BLOCK, 64), F32),
            pltpu.SemaphoreType.DMA((9,)),
        ],
        work=10**9,
    )
    messages = quad(messages)
    rights = by_slot([right] + [far(right, u) for u in range(1, groups)])

    s, og, final_t, lx, lt, gather, few = call(
        lambda *refs: adjoint_kernel(chunks, *refs),
        [
            sds((chunks * 1024, 128), BF16),
            sds((chunks * 1024, 1024), BF16),
            sds((128, 1024), BF16),
            sds((128, 1024), BF16),
            sds((1024, 128), BF16),
            sds((512, 512), BF16),
            sds(((PAIRED + EXTRA) * BLOCK, 256), BF16),
        ],
        [lengths, homologs, final, swap, spread, normed, *messages],
        in_specs=[SMEM] * 2 + [vmem()] * (4 + QUAD),
        scratch=[pltpu.VMEM(((depth + EXTRA) * BLOCK, 256), F32)],
        work=2 * 10**9,
    )

    outs = call(
        lambda *refs: grad_kernel(chunks, *refs),
        [sds((PACKED, 128), BF16)] * QUAD
        + [sds((chunks * PACKED, 128), BF16)] * 4
        + [sds((chunks * 1024, 128), BF16)],
        [lengths, og, lt, *rights[::-1]],
        in_specs=[SMEM] + [vmem()] * (2 + QUAD),
        scratch=[pltpu.VMEM((128, 1024), F32)],
        work=2 * 10**9,
    )
    lgs, rgs, rt = outs[0:4], list(outs[4:8]), outs[8]
    rgs = from_slot(rgs, PACKED)
    rgs = [rgs[0]] + [far(rgs[u], u) for u in range(1, groups)]
    own, cross, core, pair_own, pair_core, pair_cross = call(
        lambda *refs: pair_kernel(chunks, *refs),
        [sds((256 + PACKED, 128), BF16)] * 2
        + [sds((512 + 2 * PACKED, 128), BF16)]
        + [sds((groups * 64, 128), BF16)] * 2
        + [sds((groups * 128, 128), BF16)],
        [lengths, homologs, s, final_t, swap, bias, lx, rt, *lgs],
        in_specs=[SMEM] * 2 + [vmem()] * (6 + QUAD),
        scratch=[pltpu.VMEM((1024, 1024), BF16), pltpu.VMEM((1024, 128), F32)],
        work=4 * 10**9,
    )
    core = near(core, 1)
    mine, theirs = call(
        middle_kernel,
        [sds((256 + PACKED, 128), F32), sds((256 + PACKED, 128), BF16)],
        [own, cross, core],
        work=10**7,
    )
    quads = [mine, near(theirs, 2)]

    pg, fm = call(
        lambda *refs: back_kernel(groups, *refs),
        [sds(((PAIRED + EXTRA) * BLOCK, 64), BF16), sds((128, 128), BF16)],
        [gather, few, *quads, *rgs],
        scratch=[pltpu.VMEM(((PAIRED + EXTRA) * BLOCK, 64), F32)],
        work=10**9,
    )
    half = groups // 2
    w = call(fold_kernel, sds((256, 128), BF16), quads, work=10**7)
    steps = [half >> k for k in range(half.bit_length() - 1)]
    for u in steps[:-1]:
        w = call(fold_kernel, sds((256, 128), BF16), [w, far(w, u)], work=10**7)
    part = call(join_kernel, sds((384, 128), BF16), [w, far(w, steps[-1]), fm], work=10**7)
    parts = [part] + [far(part if u == 1 else fm, u) for u in range(1, groups)]
    pair_cross = near(pair_cross, 2)
    pairs = [pair_own, near(pair_core, 1), pair_cross, near(pair_cross, 1)]
    alignment_gradient = call(
        align_kernel,
        sds(x.shape, BF16),
        [lengths, homologs, pg, mat, scale, x],
        in_specs=[SMEM] * 2 + [vmem()] * 4,
        scratch=[pltpu.VMEM(((depth + EXTRA) * BLOCK, 64), F32)],
        work=10**9,
    )
    pair_delta = call(
        assemble_kernel,
        sds(adjoint.shape, BF16),
        pairs,
        scratch=[pltpu.VMEM((BLOCK * residues, 128), F32)],
        work=10**9,
    )
    parts, alignment_gradient, pair_delta = lax.optimization_barrier(
        (parts, alignment_gradient, pair_delta)
    )
    merged = call(
        merge_kernel, sds((384, 128), BF16), parts, work=10**7
    )
    cross = near(merged, 2)
    w, fm = call(
        final_kernel,
        [sds((1024, 128), F32), sds((64, 256), F32)],
        [merged, near(merged, 1), cross, near(cross, 1)],
        work=10**8,
    )
    return pair_delta, alignment_gradient, w, fm.T


def solution(mesh):
    devices = mesh.shape["row"]

    def body(*args):
        return on_device(devices, *args)

    return jax.shard_map(
        body,
        mesh=mesh,
        in_specs=(
            P("groups", "row", None),
            P(),
            P(),
            P(),
            P(),
            P(),
            P(),
            P(("groups", "row"), None, None),
            P("groups"),
            P("groups"),
        ),
        out_specs=(
            P(("groups", "row"), None, None),
            P("groups", "row", None),
            P("groups", None),
            P("groups", None),
        ),
        check_vma=False,
    )
```
